512 devices in a mesh: group: 16 (over x_lo, y, core), seq: 32 (over x_hi, z).
Axes of the slice: x: 4 (x_hi: 2, x_lo: 2; x = x_hi * 2 + x_lo), y: 4, z: 16, core: 2. Of those that a mesh axis runs over, the one named last changes fastest.
Arguments:
- queries: bfloat16 [16, 768, 4096], P('group', 'seq'), may hold values from -120 to 120
- keys: bfloat16 [16, 768, 4096], P('group', 'seq'), may hold values from -10 to 10
- values: bfloat16 [16, 768, 4096], P('group', 'seq'), may hold values from -6 to 6
- cross_queries: bfloat16 [16, 768, 4096], P('group', 'seq'), may hold values from -120 to 120
- text_keys: bfloat16 [512, 4096], P('group', 'seq'), may hold values from -10 to 10
- text_values: bfloat16 [512, 4096], P('group', 'seq'), may hold values from -6 to 6
- group_gate: float32 [16, 4096], P('group', 'seq'), may hold values from 0.5 to 1.5
- group_ids: int32 [16], replicated, may hold values from 0 to 15, each once
- text_len: int32 [1], replicated, may hold values from 256 to 512
Outputs:
- mixed: bfloat16 [16, 768, 4096], P('group', 'seq')
The draws below stay inside these ranges and needn't reach their ends.
Inputs may be any that keep to these rules, and one draw needn't show every extreme that they name: `group_ids`: every group number appears once.
All inputs are finite; a program needn't handle non-finite values.
Results may differ from the reference program's by a relative error of at most 0.009.
Values may be sent and summed in bfloat16 or wider, within the bound.
No kernel may reach another device: no remote copies, remote signals or barrier semaphores. Data moves between devices by JAX's collectives and lax.ppermute only.
A program may use at most 64 MiB of HBM per device.

```python
import math
import jax
import jax.numpy as jnp
from jax import lax

HD = 128
HEADS = 32
TEXT = 512
CT = 768
GROUPS = 16


def self_parts(key):
    shape = (GROUPS, CT, HEADS * HD)
    base = jnp.clip(1.7 * jax.random.normal(jax.random.fold_in(key, 11), shape, jnp.float32), -10.0, 10.0)
    return base


def text_parts(key):
    shape = (TEXT, HEADS * HD)
    base = jnp.clip(1.7 * jax.random.normal(jax.random.fold_in(key, 31), shape, jnp.float32), -10.0, 10.0)
    return base


def draw_keys(key, part):
    base = self_parts(key)
    return base.astype(jnp.bfloat16)


def draw_queries(key, part):
    base = self_parts(key)
    own_key = jax.random.fold_in(key, 21)
    drawn = jnp.clip(1.7 * jax.random.normal(own_key, base.shape, jnp.float32), -10.0, 10.0)
    return drawn.astype(jnp.bfloat16)


def draw_text_keys(key, part):
    base = text_parts(key)
    return base.astype(jnp.bfloat16)


def draw_cross_queries(key, part):
    own_key = jax.random.fold_in(key, 41)
    shape = (GROUPS, CT, HEADS * HD)
    drawn = jnp.clip(1.7 * jax.random.normal(own_key, shape, jnp.float32), -10.0, 10.0)
    return drawn.astype(jnp.bfloat16)


def levels(key, dims, shards, least, largest):
    factor_of = 1.0
    for position, shards_of in shards:
        draws = jax.random.uniform(jax.random.fold_in(jax.random.fold_in(key, 6), position), (shards_of,), jnp.float32, least / len(shards), largest / len(shards))
        factor_of = factor_of * jnp.repeat(jnp.exp(draws), dims[position] // shards_of).reshape((-1,) + (1,) * (len(dims) - 1 - position))
    return factor_of


def bell_draw(key, extent, scale, limit, shards=(), kind=jnp.bfloat16):
    loudness = levels(key, extent, shards, -0.22, 0.18) if shards else 1.0
    entries = jax.random.normal(key, extent, jnp.float32) * scale * loudness
    return jnp.minimum(jnp.maximum(entries, -limit), limit).astype(kind)


def setup_inputs(seed: int = 0) -> dict:
    key_list = jax.random.split(jax.random.key(seed), 10)
    return {
        "queries": draw_queries(jax.random.fold_in(key_list[9], 71), 0),
        "keys": draw_keys(jax.random.fold_in(key_list[9], 71), 0),
        "values": bell_draw(key_list[2], (GROUPS, CT, HEADS * HD), 1.0, 6.0, ((0, 16), (1, 32))),
        "cross_queries": draw_cross_queries(jax.random.fold_in(key_list[9], 71), 0),
        "text_keys": draw_text_keys(jax.random.fold_in(key_list[9], 71), 0),
        "text_values": bell_draw(key_list[5], (TEXT, HEADS * HD), 1.0, 6.0, ((0, 16), (1, 32))),
        "group_gate": jnp.clip(0.5 + 1.0 * jax.random.uniform(key_list[6], (GROUPS, HEADS * HD), jnp.float32) ** levels(key_list[6], (GROUPS, HEADS * HD), ((0, 16), (1, 32)), -0.2, 0.2), 0.5, 1.5),
        "group_ids": jax.random.permutation(key_list[7], GROUPS).astype(jnp.int32),
        "text_len": jax.random.randint(key_list[8], (1,), TEXT // 2, TEXT + 1).astype(jnp.int32),
    }


def attend(query_rows, key_rows, value_rows, visible):
    scores = jnp.dot(query_rows, key_rows.T, preferred_element_type=jnp.float32) * (1.0 / math.sqrt(HD))
    scores = jnp.where(visible[None, :], scores, -jnp.inf)
    row_top = lax.optimization_barrier(jnp.max(scores, axis=1, keepdims=True))
    weights = jnp.exp(scores - row_top)
    totals = lax.optimization_barrier(jnp.sum(weights, axis=1, keepdims=True))
    return jnp.dot(weights.astype(jnp.bfloat16), value_rows, preferred_element_type=jnp.float32) / totals

def head_major(array, row_count):
    return jnp.transpose(array.reshape(row_count, HEADS, HD), (1, 0, 2))

def reference(queries, keys, values, cross_queries, text_keys, text_values, group_gate, group_ids, text_len):
    group_count = queries.shape[0]
    row_count = queries.shape[1]
    ranks = jnp.arange(group_count, dtype=jnp.int32)
    slot_of = lax.optimization_barrier(jnp.sum(jnp.where(group_ids[None, :] == ranks[:, None], ranks[None, :], 0), axis=1)).astype(jnp.int32)
    ordered_keys = head_major(jnp.take(keys, slot_of, axis=0), group_count * row_count)
    ordered_values = head_major(jnp.take(values, slot_of, axis=0), group_count * row_count)
    text_key_heads = head_major(text_keys, TEXT)
    text_value_heads = head_major(text_values, TEXT)
    text_visible = jnp.arange(TEXT, dtype=jnp.int32) < text_len[0]
    outputs = jnp.zeros(queries.shape, jnp.bfloat16)
    for rank_index in range(group_count):
        slot_index = slot_of[rank_index]
        prefix = (rank_index + 1) * row_count
        own_query = head_major(lax.dynamic_index_in_dim(queries, slot_index, 0, keepdims=False), row_count)
        own_cross = head_major(lax.dynamic_index_in_dim(cross_queries, slot_index, 0, keepdims=False), row_count)
        own_gate = lax.dynamic_index_in_dim(group_gate, slot_index, 0, keepdims=False).reshape(HEADS, HD)
        visible = jnp.ones((prefix,), dtype=jnp.bool_)

        def per_head(operands):
            head_query, head_keys, head_values, head_cross, head_text_keys, head_text_values, head_gate = operands
            self_part = attend(head_query, head_keys, head_values, visible)
            cross_part = attend(head_cross, head_text_keys, head_text_values, text_visible)
            return (head_gate[None, :] * self_part + cross_part).astype(jnp.bfloat16)
        per_heads = lax.map(per_head, (own_query, ordered_keys[:, :prefix], ordered_values[:, :prefix], own_cross, text_key_heads, text_value_heads, own_gate))
        block_rows = jnp.transpose(per_heads, (1, 0, 2)).reshape(row_count, HEADS * HD)
        outputs = lax.dynamic_update_index_in_dim(outputs, block_rows, slot_index, 0)
    return outputs
```

```python
import functools
import math

import jax
import jax.numpy as jnp
from jax import lax
from jax.experimental import pallas as pl
from jax.experimental.pallas import tpu as pltpu
from jax.sharding import PartitionSpec as P

HD = 128
LOG2 = math.log2(math.e) / math.sqrt(HD)
LOW = -1e30
VMEM = pl.BlockSpec(memory_space=pltpu.VMEM)
SMEM = pl.BlockSpec(memory_space=pltpu.SMEM)
PARAMS = pltpu.CompilerParams(vmem_limit_bytes=40 * 2**20)


def core_of(i):
    return i + 1 - 2 * (i % 2)


def across_x(i):
    return (i + 8) % 16


def across_y1(i):
    y = (i // 2) % 4
    return i + 2 * (1 - 2 * (y % 2))


def across_y2(i):
    y = (i // 2) % 4
    return (i // 8) * 8 + ((y + 2 * (y % 2) + 3) % 4) * 2 + i % 2


def across_xy2(i):
    return across_x(across_y2(i))


def swap(array, partner):
    return lax.ppermute(array, "group", [(i, partner(i)) for i in range(16)])


def pack_kernel(q_ref, k_ref, v_ref, c_ref, out_ref):
    for head in range(out_ref.shape[0]):
        for slot, ref in enumerate((q_ref, k_ref, v_ref, c_ref)):
            out_ref[head, slot] = ref[0, :, head * HD : (head + 1) * HD]


def pack(queries, keys, values, cross_queries):
    rows, width = queries.shape[1:]
    return pl.pallas_call(
        pack_kernel,
        in_specs=[VMEM] * 4,
        out_specs=VMEM,
        out_shape=jax.ShapeDtypeStruct((width // HD, 4, rows, HD), jnp.bfloat16),
        compiler_params=PARAMS,
        name="pack",
    )(queries, keys, values, cross_queries)


def unpack_kernel(in_ref, q_ref, kv_ref, c_ref):
    for part in range(in_ref.shape[0]):
        q_ref[part] = in_ref[part, 0]
        kv_ref[0, part] = in_ref[part, 1]
        kv_ref[1, part] = in_ref[part, 2]
        c_ref[part] = in_ref[part, 3]


def unpack(received):
    parts, _, rows, width = received.shape
    one = jax.ShapeDtypeStruct((parts, rows, width), jnp.bfloat16)
    two = jax.ShapeDtypeStruct((2, parts, rows, width), jnp.bfloat16)
    q, kv, c = pl.pallas_call(
        unpack_kernel,
        in_specs=[VMEM],
        out_specs=[VMEM] * 3,
        out_shape=[one, two, one],
        compiler_params=PARAMS,
        name="unpack",
    )(received)
    count = parts * rows
    return q.reshape(count, width), kv.reshape(2, count, width), c.reshape(count, width)


def scores_of(q, k):
    return lax.dot_general(
        q, k, (((1,), (1,)), ((), ())), preferred_element_type=jnp.float32
    )


def with_ones(v):
    return jnp.concatenate([v, jnp.ones_like(v)], axis=1)


def attend(q_ref, k, v, top_ref, sum_ref, tile, mask=None):
    v = with_ones(v)
    count = q_ref.shape[0] // tile

    def soft(step, s):
        rows = pl.ds(step * tile, tile)
        if mask is not None:
            s = jnp.where(mask, s, LOW)
        old = top_ref[rows, :]
        new = jnp.maximum(old, jnp.max(s, axis=1, keepdims=True))
        p = jnp.exp2((s - new[:, :1]) * LOG2).astype(jnp.bfloat16)
        factor = jnp.exp2((old - new) * LOG2)
        top_ref[rows, :] = new
        return rows, p, jnp.concatenate([factor, factor], axis=1)

    def mix(rows, p, factor):
        sum_ref[rows, :] = sum_ref[rows, :] * factor + jnp.dot(
            p, v, preferred_element_type=jnp.float32
        )

    s = scores_of(q_ref[pl.ds(0, tile), :], k)
    last = None
    for step in range(count):
        ahead = None
        if step + 1 < count:
            ahead = scores_of(q_ref[pl.ds((step + 1) * tile, tile), :], k)
        now = soft(step, s)
        if last is not None:
            mix(*last)
        last, s = now, ahead
    mix(*last)


def attend_pair(q_ref, one_ref, two_ref, see_one, see_two, top_ref, sum_ref):
    @pl.when(see_one & see_two)
    def _():
        k = jnp.concatenate([one_ref[0], two_ref[0]], axis=0)
        v = jnp.concatenate([one_ref[1], two_ref[1]], axis=0)
        attend(q_ref, k, v, top_ref, sum_ref, 256)

    @pl.when(see_one & jnp.logical_not(see_two))
    def _():
        attend(q_ref, one_ref[0], one_ref[1], top_ref, sum_ref, 256)

    @pl.when(see_two & jnp.logical_not(see_one))
    def _():
        attend(q_ref, two_ref[0], two_ref[1], top_ref, sum_ref, 256)


def self_part(whose, ids_ref, q_ref, a0, a1, b0, b1, top_ref, sum_ref):
    slot = lax.axis_index("group")
    rank = ids_ref[whose(slot)]
    near = across_y1(slot)
    see = [ids_ref[j] <= rank for j in (slot, core_of(slot), near, core_of(near))]
    top_ref[...] = jnp.full_like(top_ref, LOW)
    sum_ref[...] = jnp.zeros_like(sum_ref)
    attend_pair(q_ref, a0, a1, see[0], see[1], top_ref, sum_ref)
    attend_pair(q_ref, b0, b1, see[2], see[3], top_ref, sum_ref)


def log_sums(top_ref, sum_ref):
    lines = []
    for step in range(top_ref.shape[0] // HD):
        rows = pl.ds(step * HD, HD)
        total = sum_ref[rows, HD:]
        line = jnp.where(total > 0, jnp.log2(total) + top_ref[rows, :] * LOG2, LOW)
        lines.append(line.T[0:1, :])
    lines.append(jnp.full((8 - len(lines), HD), LOW, jnp.float32))
    return jnp.concatenate(lines, axis=0)


def mean_of(sum_ref):
    total = sum_ref[:, HD:]
    return sum_ref[:, :HD] / jnp.where(total > 0, total, 1.0)


def other_kernel(whose, ids_ref, q_ref, a0, a1, b0, b1, out_ref, top_ref, sum_ref):
    self_part(whose, ids_ref, q_ref, a0, a1, b0, b1, top_ref, sum_ref)
    count = q_ref.shape[0]
    out_ref[pl.ds(0, count), :] = mean_of(sum_ref).astype(jnp.bfloat16)
    logs = log_sums(top_ref, sum_ref)
    high = logs.astype(jnp.bfloat16)
    rest = logs - high.astype(jnp.float32)
    mid = rest.astype(jnp.bfloat16)
    low = (rest - mid.astype(jnp.float32)).astype(jnp.bfloat16)
    tail = jnp.concatenate([high, mid, low, jnp.zeros_like(low)], axis=0)
    out_ref[pl.ds(count, 32), :] = tail


def own_kernel(
    ids_ref, len_ref, q_ref, a0, a1, b0, b1, c_ref, text_ref,
    mean_ref, logs_ref, cross_ref, top_ref, sum_ref,
):
    top_ref[...] = jnp.full_like(top_ref, LOW)
    sum_ref[...] = jnp.zeros_like(sum_ref)
    texts = text_ref.shape[0] * text_ref.shape[2]
    mask = lax.broadcasted_iota(jnp.int32, (1, texts), 1) < len_ref[0]
    attend(
        c_ref,
        text_ref[:, 0].reshape(texts, HD),
        text_ref[:, 1].reshape(texts, HD),
        top_ref,
        sum_ref,
        256,
        mask,
    )
    cross_ref[...] = mean_of(sum_ref)
    self_part(lambda i: i, ids_ref, q_ref, a0, a1, b0, b1, top_ref, sum_ref)
    mean_ref[...] = mean_of(sum_ref)
    logs_ref[...] = log_sums(top_ref, sum_ref)


def scratch(count):
    return [
        pltpu.VMEM((count, HD), jnp.float32),
        pltpu.VMEM((count, 2 * HD), jnp.float32),
    ]


COST = pl.CostEstimate(
    flops=16 * 768 * 768 * 128, bytes_accessed=2**21, transcendentals=4 * 768 * 768
)


def other(whose, group_ids, q, blocks):
    count = q.shape[0]
    return pl.pallas_call(
        functools.partial(other_kernel, whose),
        in_specs=[SMEM] + [VMEM] * 5,
        out_specs=VMEM,
        out_shape=jax.ShapeDtypeStruct((count + 32, HD), jnp.bfloat16),
        scratch_shapes=scratch(count),
        compiler_params=PARAMS,
        cost_estimate=COST,
        name="other",
    )(group_ids, q, *blocks)


def own(group_ids, text_len, q, blocks, cross, text):
    count = q.shape[0]
    full = jax.ShapeDtypeStruct((count, HD), jnp.float32)
    return pl.pallas_call(
        own_kernel,
        in_specs=[SMEM] * 2 + [VMEM] * 7,
        out_specs=[VMEM] * 3,
        out_shape=[full, jax.ShapeDtypeStruct((8, HD), jnp.float32), full],
        scratch_shapes=scratch(count),
        compiler_params=PARAMS,
        cost_estimate=COST,
        name="own",
    )(group_ids, text_len, q, *blocks, cross, text)


def merge_kernel(mean_ref, logs_ref, cross_ref, r0, r1, r2, gate_ref, out_ref):
    count = mean_ref.shape[0]
    logs = [logs_ref[...]]
    for ref in (r0, r1, r2):
        tail = ref[pl.ds(count, 32), :].astype(jnp.float32)
        logs.append(tail[0:8] + tail[8:16] + tail[16:24])
    best = functools.reduce(jnp.maximum, logs)
    weights = [jnp.exp2(line - best) for line in logs]
    total = functools.reduce(jnp.add, weights)
    weights = [w / total for w in weights]
    gate = gate_ref[...]
    for step in range(count // HD):
        rows = pl.ds(step * HD, HD)
        parts = [mean_ref[rows, :]]
        parts += [ref[rows, :].astype(jnp.float32) for ref in (r0, r1, r2)]
        mixed = None
        for w, part in zip(weights, parts):
            column = jnp.broadcast_to(w[step : step + 1, :], (HD, HD)).T
            mixed = column * part if mixed is None else mixed + column * part
        out_ref[rows, :] = (gate * mixed + cross_ref[rows, :]).astype(jnp.bfloat16)


def merge(mean, logs, cross, received, gate):
    return pl.pallas_call(
        merge_kernel,
        in_specs=[VMEM] * 7,
        out_specs=VMEM,
        out_shape=jax.ShapeDtypeStruct(mean.shape, jnp.bfloat16),
        compiler_params=PARAMS,
        name="merge",
    )(mean, logs, cross, *received, gate)


def gather_text(text_keys, text_values):
    both = jnp.stack([text_keys, text_values])
    return lax.all_gather(both, "group", axis=0)


def body(
    queries, keys, values, cross_queries, text_keys, text_values, group_gate, group_ids, text_len
):
    text = gather_text(text_keys, text_values)
    packed = pack(queries, keys, values, cross_queries)
    received = lax.all_to_all(packed, "seq", split_axis=0, concat_axis=0, tiled=True)
    q, kv, cross = unpack(received)
    kv_near = swap(kv, across_y1)
    q_xy, q_x, q_y = swap(q, across_xy2), swap(q, across_x), swap(q, across_y2)
    blocks = [kv, swap(kv, core_of), kv_near, swap(kv_near, core_of)]
    back = []
    for whose, rows in ((across_xy2, q_xy), (across_x, q_x), (across_y2, q_y)):
        back.append(swap(other(whose, group_ids, rows, blocks), whose))
    mean, logs, crossed = own(group_ids, text_len, q, blocks, cross, text)
    mixed = merge(mean, logs, crossed, back, group_gate)
    count = mixed.shape[0]
    heads = lax.axis_size("seq")
    mixed = lax.all_to_all(
        mixed.reshape(heads, count // heads, HD), "seq", split_axis=0, concat_axis=0, tiled=True
    )
    return jnp.transpose(mixed, (1, 0, 2)).reshape(1, count // heads, heads * HD)


def solution(mesh):
    return jax.shard_map(
        body,
        mesh=mesh,
        in_specs=(
            P("group", "seq", None),
            P("group", "seq", None),
            P("group", "seq", None),
            P("group", "seq", None),
            P("group", "seq"),
            P("group", "seq"),
            P("group", "seq"),
            P(),
            P(),
        ),
        out_specs=P("group", "seq", None),
        check_vma=False,
    )
```

```python
import functools
import math

import jax
import jax.numpy as jnp
from jax import lax
from jax.experimental import pallas as pl
from jax.experimental.pallas import tpu as pltpu
from jax.sharding import PartitionSpec as P

HD = 128
LOG2 = math.log2(math.e) / math.sqrt(HD)
LOW = -1e30
VMEM = pl.BlockSpec(memory_space=pltpu.VMEM)
SMEM = pl.BlockSpec(memory_space=pltpu.SMEM)
PARAMS = pltpu.CompilerParams(vmem_limit_bytes=24 * 2**20)


SMALL, LARGE = 2.0**-60, 2.0**90
TILE = 384


def core_of(i):
    return i + 1 - 2 * (i % 2)


def across_x(i):
    return (i + 8) % 16


def across_y1(i):
    y = (i // 2) % 4
    return i + 2 * (1 - 2 * (y % 2))


def across_y2(i):
    y = (i // 2) % 4
    return (i // 8) * 8 + ((y + 2 * (y % 2) + 3) % 4) * 2 + i % 2


def across_xy2(i):
    return across_x(across_y2(i))


def swap(array, partner):
    return lax.ppermute(array, "group", [(i, partner(i)) for i in range(16)])


CHUNKS = 4


def pack_kernel(q_hbm, k_hbm, v_hbm, c_hbm, out_ref, held, sems):
    sources = (q_hbm, k_hbm, v_hbm, c_hbm)
    heads = out_ref.shape[0]
    chunk = heads // CHUNKS * HD
    copies = []
    for slot, ref in enumerate(sources):
        for part in range(CHUNKS):
            where = pl.ds(part * chunk, chunk)
            copy = pltpu.make_async_copy(
                ref.at[0, :, where], held.at[slot, :, where], sems.at[slot, part]
            )
            copy.start()
            copies.append(copy)
    for slot in range(len(sources)):
        for part in range(CHUNKS):
            copies[slot * CHUNKS + part].wait()
            for head in range(part * heads // CHUNKS, (part + 1) * heads // CHUNKS):
                out_ref[head, slot] = held[slot, :, head * HD : (head + 1) * HD]


def pack(queries, keys, values, cross_queries):
    rows, width = queries.shape[1:]
    heads = width // HD
    return pl.pallas_call(
        pack_kernel,
        in_specs=[pl.BlockSpec(memory_space=pl.ANY)] * 4,
        out_specs=VMEM,
        out_shape=jax.ShapeDtypeStruct((heads, 4, rows, HD), jnp.bfloat16),
        scratch_shapes=[
            pltpu.VMEM((4, rows, width), jnp.bfloat16),
            pltpu.SemaphoreType.DMA((4, CHUNKS)),
        ],
        compiler_params=pltpu.CompilerParams(vmem_limit_bytes=56 * 2**20),
        name="pack",
    )(queries, keys, values, cross_queries)


def unpack_kernel(in_ref, tk_ref, tv_ref, gate_in, q_ref, kv_ref, c_ref, gate_ref, v_ref):
    gate_ref[...] = gate_in[...]
    parts, _, rows, _ = in_ref.shape
    count = parts * rows

    @pl.loop(0, parts // 2)
    def _(part):
        pair = pl.ds(pl.multiple_of(part * 2 * rows, 16), 2 * rows)

        def both(slot):
            return jnp.concatenate(
                [in_ref[2 * part, slot], in_ref[2 * part + 1, slot]], axis=0
            )

        q_ref[pair, :] = both(0)
        kv_ref[0, pair, :] = both(1)
        v_ref[pair, :] = both(2)
        c_ref[pair, :] = both(3)

    @pl.loop(0, count // HD)
    def _(block):
        where = pl.ds(pl.multiple_of(block * HD, HD), HD)
        kv_ref[1, where, :] = v_ref[where, :].T

    tail = pl.ds(count, tk_ref.shape[0])
    kv_ref[0, tail, :] = tk_ref[...]
    kv_ref[1, tail, :] = tv_ref[...]


def unpack(received, text_keys, text_values, gate):
    parts, _, rows, width = received.shape
    count = parts * rows
    one = jax.ShapeDtypeStruct((count, width), jnp.bfloat16)
    two = jax.ShapeDtypeStruct((2, count + text_keys.shape[0], width), jnp.bfloat16)
    return pl.pallas_call(
        unpack_kernel,
        in_specs=[VMEM] * 4,
        out_specs=[VMEM] * 4,
        out_shape=[one, two, one, jax.ShapeDtypeStruct(gate.shape, gate.dtype)],
        scratch_shapes=[pltpu.VMEM((count, width), jnp.bfloat16)],
        compiler_params=PARAMS,
        name="unpack",
    )(received, text_keys, text_values, gate)


def join_kernel(a_ref, b_ref, out_ref):
    @pl.loop(0, a_ref.shape[0] // 32)
    def _(step):
        rows = pl.ds(pl.multiple_of(step * 32, 32), 32)
        out_ref[0, rows, :] = a_ref[rows, :]
        out_ref[1, rows, :] = b_ref[rows, :]


def join(a, b):
    rows = a.size // HD
    out = pl.pallas_call(
        join_kernel,
        in_specs=[VMEM] * 2,
        out_specs=VMEM,
        out_shape=jax.ShapeDtypeStruct((2, rows, HD), a.dtype),
        compiler_params=PARAMS,
        name="join",
    )(a.reshape(rows, HD), b.reshape(rows, HD))
    return out.reshape((2,) + a.shape)


def scores_of(k, q):
    return lax.dot_general(
        k, q, (((1,), (1,)), ((), ())), preferred_element_type=jnp.float32
    )


def with_ones(v):
    return jnp.concatenate([v, jnp.ones((16, v.shape[1]), v.dtype)], axis=0)


def features_first(v_blocks):
    count = v_blocks.shape[0] // HD
    return jnp.concatenate([v_blocks[i * HD : (i + 1) * HD] for i in range(count)], axis=1)


def key_groups(slot):
    near = across_y1(slot)
    return slot, core_of(slot), near, core_of(near)


def self_part(ids_ref, sources, mine, theirs, refs):
    q_ref, k_ref, v_ref, top_ref, sum_ref, s_even, s_odd, list_ref = refs
    slot = lax.axis_index("group")
    count = k_ref.shape[1]
    halves = count // TILE
    for place, (_, ref) in enumerate(sources):
        q_ref[place] = ref[...]

    @pl.loop(0, 2)
    def _(side):
        for place, ref in enumerate((mine, theirs)):
            k_ref[2 * side + place] = ref[side, 0, pl.ds(0, count), :]
            v_ref[2 * side + place] = with_ones(
                features_first(ref[side, 1, pl.ds(0, count), :])
            )

    def queries(place, half):
        return q_ref[place, pl.ds(half * TILE, TILE), :]

    @pl.loop(0, len(sources))
    def _(place):
        for half in range(halves):
            s = scores_of(k_ref[0, pl.ds(0, HD), :], queries(place, half))
            top_ref[place, half] = jnp.max(s, axis=0, keepdims=True)
            sum_ref[place, half] = jnp.zeros_like(sum_ref[place, half])

    list_ref[0] = 0
    length = jnp.int32(0)
    seen = []
    for place, (owner, _) in enumerate(sources):
        rank = ids_ref[owner(slot)]
        before = length
        for number, group in enumerate(key_groups(slot)):
            list_ref[length] = 4 * place + number
            length = length + (ids_ref[group] <= rank).astype(jnp.int32)
        seen.append(length > before)

    def mix(place, number, half, s):
        p = jnp.exp2((s - top_ref[place, half]) * LOG2).astype(jnp.bfloat16)
        sum_ref[place, half] += jnp.dot(
            v_ref[number], p, preferred_element_type=jnp.float32
        )

    def item(index):
        code = list_ref[index]
        return code // 4, code % 4

    place, number = item(0)
    s_even[...] = scores_of(k_ref[number], queries(place, 0))

    @pl.loop(0, length)
    def _(index):
        place, number = item(index)
        s_odd[...] = scores_of(k_ref[number], queries(place, 1))
        mix(place, number, 0, s_even[...])
        next_place, next_number = item(jnp.minimum(index + 1, length - 1))
        s_even[...] = scores_of(k_ref[next_number], queries(next_place, 0))
        mix(place, number, 1, s_odd[...])

    inside = jnp.bool_(True)
    for place, some in enumerate(seen):
        totals = sum_ref[place, :, HD : HD + 1, :]
        good = (jnp.min(totals) > SMALL) & (jnp.max(totals) < LARGE)
        inside = inside & (good | jnp.logical_not(some))

    @pl.when(jnp.logical_not(inside))
    def _():
        top_ref[...] = jnp.full_like(top_ref, LOW)
        sum_ref[...] = jnp.zeros_like(sum_ref)

        @pl.loop(0, length * halves)
        def _(index):
            place, number = item(index // halves)
            half = index % halves
            where = pl.ds(pl.multiple_of(half * TILE, TILE), TILE)
            s = scores_of(k_ref[number], q_ref[place, where, :])
            old = top_ref[place, half]
            new = jnp.maximum(old, jnp.max(s, axis=0, keepdims=True))
            top_ref[place, half] = new
            sum_ref[place, half] = sum_ref[place, half] * jnp.exp2((old - new) * LOG2)
            mix(place, number, half, s)


def log_sums(place, top_ref, sum_ref):
    lines = []
    for half in range(top_ref.shape[1]):
        total = sum_ref[place, half, HD : HD + 1, :]
        logs = jnp.where(total > 0, jnp.log2(total) + top_ref[place, half] * LOG2, LOW)
        lines += [logs[:, start : start + HD] for start in range(0, TILE, HD)]
    lines.append(jnp.full((8 - len(lines), HD), LOW, jnp.float32))
    return jnp.concatenate(lines, axis=0)


def means(sums, write):
    for start in range(0, TILE, HD):
        total = sums[HD : HD + 1, start : start + HD]
        part = sums[:HD, start : start + HD] / jnp.where(total > 0, total, 1.0)
        write(start, part.T)


OTHERS = (across_x, across_y2, across_xy2)


def others_kernel(ids_ref, x_ref, y_ref, mine, theirs, out_x, out_y, out_xy, *refs):
    queries = (x_ref, y_ref.at[0], y_ref.at[1])
    self_part(ids_ref, list(zip(OTHERS, queries)), mine, theirs, refs)
    top_ref, sum_ref = refs[3:5]
    count = x_ref.shape[0]
    texts = mine.shape[2] - count
    for place, out_ref in enumerate((out_x, out_y, out_xy)):

        @pl.loop(0, count // TILE)
        def _(half):
            def write(start, part):
                where = pl.ds(pl.multiple_of(half * TILE + start, HD), HD)
                out_ref[where, :] = part.astype(jnp.bfloat16)

            means(sum_ref[place, half], write)

        logs = log_sums(place, top_ref, sum_ref)
        high = logs.astype(jnp.bfloat16)
        rest = logs - high.astype(jnp.float32)
        mid = rest.astype(jnp.bfloat16)
        low = (rest - mid.astype(jnp.float32)).astype(jnp.bfloat16)
        tail = jnp.concatenate([high, mid, low, jnp.zeros_like(low)], axis=0)
        out_ref[pl.ds(count, 32), :] = tail
        for piece in range(8):
            ref = (mine, theirs)[piece // 2 % 2]
            text = ref[piece // 4, piece % 2, pl.ds(count, texts), :]
            out_ref[pl.ds(count + 32 + piece * texts, texts), :] = text


def own_kernel(ids_ref, q_ref, mine, theirs, mean_ref, logs_ref, *refs):
    self_part(ids_ref, [(lambda i: i, q_ref)], mine, theirs, refs)
    top_ref, sum_ref = refs[3:5]

    @pl.loop(0, q_ref.shape[0] // TILE)
    def _(half):
        def write(start, part):
            where = pl.ds(pl.multiple_of(half * TILE + start, HD), HD)
            mean_ref[where, :] = part

        means(sum_ref[0, half], write)

    logs_ref[...] = log_sums(0, top_ref, sum_ref)


def scratch(places, count):
    halves = count // TILE
    return [
        pltpu.VMEM((places, count, HD), jnp.bfloat16),
        pltpu.VMEM((4, count, HD), jnp.bfloat16),
        pltpu.VMEM((4, HD + 16, count), jnp.bfloat16),
        pltpu.VMEM((places, halves, 1, TILE), jnp.float32),
        pltpu.VMEM((places, halves, HD + 16, TILE), jnp.float32),
        pltpu.VMEM((count, TILE), jnp.float32),
        pltpu.VMEM((count, TILE), jnp.float32),
        pltpu.SMEM((4 * places + 1,), jnp.int32),
    ]


def cost(parts):
    return pl.CostEstimate(
        flops=parts * 16 * 768 * 768 * 128,
        bytes_accessed=parts * 2**21,
        transcendentals=parts * 4 * 768 * 768,
    )


def others(group_ids, q_x, q_y, mine, theirs):
    count = q_x.shape[0]
    texts = 8 * (mine.shape[2] - count)
    out = jax.ShapeDtypeStruct((count + 32 + texts, HD), jnp.bfloat16)
    return pl.pallas_call(
        others_kernel,
        in_specs=[SMEM] + [VMEM] * 4,
        out_specs=[VMEM] * 3,
        out_shape=[out] * 3,
        scratch_shapes=scratch(3, count),
        compiler_params=PARAMS,
        cost_estimate=cost(3),
        name="others",
    )(group_ids, q_x, q_y, mine, theirs)


def own(group_ids, q, mine, theirs):
    count = q.shape[0]
    return pl.pallas_call(
        own_kernel,
        in_specs=[SMEM] + [VMEM] * 3,
        out_specs=[VMEM] * 2,
        out_shape=[
            jax.ShapeDtypeStruct((count, HD), jnp.float32),
            jax.ShapeDtypeStruct((8, HD), jnp.float32),
        ],
        scratch_shapes=scratch(1, count),
        compiler_params=PARAMS,
        cost_estimate=cost(1),
        name="own",
    )(group_ids, q, mine, theirs)


def merge_kernel(
    len_ref, mean_ref, logs_ref, c_ref, mine, theirs, r0, r1, r2, gate_ref,
    out_ref, tk_ref, tv_ref, cross_ref, weight_ref,
):
    count = mean_ref.shape[0]
    pieces, texts, _ = tk_ref.shape
    slot = lax.axis_index("group")
    for side, held in enumerate((tk_ref, tv_ref)):
        for place, group in enumerate(key_groups(slot)):
            ref = (mine, theirs)[place % 2]
            held[group] = ref[place // 2, side, pl.ds(count, texts), :]
        for whose, ref in zip(OTHERS, (r0, r1, r2)):
            for place, group in enumerate(key_groups(whose(slot))):
                start = count + 32 + (2 * place + side) * texts
                held[group] = ref[pl.ds(start, texts), :]
    length = pieces * texts
    mask = lax.broadcasted_iota(jnp.int32, (length, 1), 0) < len_ref[0]
    k = tk_ref[...].reshape(length, HD)
    v = with_ones(tv_ref[...].reshape(length, HD).T)

    @pl.loop(0, count // TILE)
    def _(half):
        queries = c_ref[pl.ds(pl.multiple_of(half * TILE, TILE), TILE), :]
        s = jnp.where(mask, scores_of(k, queries), LOW)
        top = jnp.max(s, axis=0, keepdims=True)
        p = jnp.exp2((s - top) * LOG2).astype(jnp.bfloat16)
        sums = jnp.dot(v, p, preferred_element_type=jnp.float32)

        def write(start, part):
            cross_ref[pl.ds(pl.multiple_of(half * TILE + start, HD), HD), :] = part

        means(sums, write)

    logs = [logs_ref[...]]
    for ref in (r0, r1, r2):
        tail = ref[pl.ds(count, 32), :].astype(jnp.float32)
        logs.append(tail[0:8] + tail[8:16] + tail[16:24])
    best = functools.reduce(jnp.maximum, logs)
    weights = [jnp.exp2(line - best) for line in logs]
    total = functools.reduce(jnp.add, weights)
    for place, weight in enumerate(weights):
        weight_ref[place] = weight / total
    gate = gate_ref[...]

    @pl.loop(0, count // HD)
    def _(step):
        rows = pl.ds(pl.multiple_of(step * HD, HD), HD)
        parts = [mean_ref[rows, :]]
        parts += [ref[rows, :].astype(jnp.float32) for ref in (r0, r1, r2)]
        mixed = None
        for place, part in enumerate(parts):
            line = weight_ref[place, pl.ds(step, 1), :]
            column = jnp.broadcast_to(line, (HD, HD)).T
            mixed = column * part if mixed is None else mixed + column * part
        out_ref[rows, :] = (gate * mixed + cross_ref[rows, :]).astype(jnp.bfloat16)


def merge(text_len, mean, logs, cross, mine, theirs, received, gate):
    count = cross.shape[0]
    held = pltpu.VMEM((16, mine.shape[2] - count, HD), jnp.bfloat16)
    return pl.pallas_call(
        merge_kernel,
        in_specs=[SMEM] + [VMEM] * 9,
        out_specs=VMEM,
        out_shape=jax.ShapeDtypeStruct(mean.shape, jnp.bfloat16),
        scratch_shapes=[
            held,
            held,
            pltpu.VMEM((count, HD), jnp.float32),
            pltpu.VMEM((4, 8, HD), jnp.float32),
        ],
        compiler_params=PARAMS,
        cost_estimate=cost(1),
        name="merge",
    )(text_len, mean, logs, cross, mine, theirs, *received, gate)


def to_heads(array):
    return lax.all_to_all(array, "seq", split_axis=0, concat_axis=0, tiled=True)


def body(
    queries, keys, values, cross_queries, text_keys, text_values, group_gate, group_ids, text_len
):
    packed = pack(queries, keys, values, cross_queries)
    received = to_heads(packed)
    q, kv, cross, gate = unpack(received, text_keys, text_values, group_gate)
    kv_near, q_x = lax.optimization_barrier((swap(kv, across_y1), swap(q, across_x)))
    mine = join(kv, kv_near)
    q_y = swap(join(q, q_x), across_y2)
    theirs = swap(mine, core_of)
    sent = others(group_ids, q_x, q_y, mine, theirs)
    back = [swap(one, whose) for one, whose in zip(sent, OTHERS)]
    mean, logs = own(group_ids, q, mine, theirs)
    mixed = merge(text_len, mean, logs, cross, mine, theirs, back, gate)
    count = mixed.shape[0]
    heads = lax.axis_size("seq")
    mixed = to_heads(mixed.reshape(heads, count // heads, HD))
    return jnp.transpose(mixed, (1, 0, 2)).reshape(1, count // heads, heads * HD)


def solution(mesh):
    return jax.shard_map(
        body,
        mesh=mesh,
        in_specs=(
            P("group", "seq", None),
            P("group", "seq", None),
            P("group", "seq", None),
            P("group", "seq", None),
            P("group", "seq"),
            P("group", "seq"),
            P("group", "seq"),
            P(),
            P(),
        ),
        out_specs=P("group", "seq", None),
        check_vma=False,
    )
```

```python
import functools
import math

import jax
import jax.numpy as jnp
from jax import lax
from jax.experimental import pallas as pl
from jax.experimental.pallas import tpu as pltpu
from jax.sharding import PartitionSpec as P

HD = 128
LOG2 = math.log2(math.e) / math.sqrt(HD)
LOW = -1e30
VMEM = pl.BlockSpec(memory_space=pltpu.VMEM)
SMEM = pl.BlockSpec(memory_space=pltpu.SMEM)
PARAMS = pltpu.CompilerParams(vmem_limit_bytes=14 * 2**20)


SMALL, LARGE = 2.0**-60, 2.0**90
TILE = 384


def core_of(i):
    return i + 1 - 2 * (i % 2)


def across_x(i):
    return (i + 8) % 16


def across_y1(i):
    y = (i // 2) % 4
    return i + 2 * (1 - 2 * (y % 2))


def across_y2(i):
    y = (i // 2) % 4
    return (i // 8) * 8 + ((y + 2 * (y % 2) + 3) % 4) * 2 + i % 2


def across_xy2(i):
    return across_x(across_y2(i))


CLUSTERS = [
    [i, across_x(i), across_y2(i), across_xy2(i)] for i in (2, 3, 6, 7)
]
OWNERS = (lambda i: i, across_x, across_y2, across_xy2)


def place_of(i):
    y = (i // 2) % 4
    return i // 8 + 2 * ((y + 1) % 2)


def place_across(i, step):
    place = place_of(i)
    x, y = place % 2, place // 2
    if step % 2:
        x = 1 - x
    if step // 2:
        y = 1 - y
    return x + 2 * y


def in_cluster(array):
    return lax.all_to_all(
        array, "group", split_axis=0, concat_axis=0, axis_index_groups=CLUSTERS, tiled=True
    )


def swap(array, partner):
    return lax.ppermute(array, "group", [(i, partner(i)) for i in range(16)])


CHUNKS = 4


def pack_kernel(q_hbm, k_hbm, v_hbm, c_hbm, out_ref, held, sems):
    sources = (q_hbm, k_hbm, v_hbm, c_hbm)
    heads = out_ref.shape[0]
    chunk = heads // CHUNKS * HD
    copies = []
    for slot, ref in enumerate(sources):
        for part in range(CHUNKS):
            where = pl.ds(part * chunk, chunk)
            copy = pltpu.make_async_copy(
                ref.at[0, :, where], held.at[slot, :, where], sems.at[slot, part]
            )
            copy.start()
            copies.append(copy)
    for slot in range(len(sources)):
        for part in range(CHUNKS):
            copies[slot * CHUNKS + part].wait()
            for head in range(part * heads // CHUNKS, (part + 1) * heads // CHUNKS):
                out_ref[head, slot] = held[slot, :, head * HD : (head + 1) * HD]


def pack(queries, keys, values, cross_queries):
    rows, width = queries.shape[1:]
    heads = width // HD
    return pl.pallas_call(
        pack_kernel,
        in_specs=[pl.BlockSpec(memory_space=pl.ANY)] * 4,
        out_specs=VMEM,
        out_shape=jax.ShapeDtypeStruct((heads, 4, rows, HD), jnp.bfloat16),
        scratch_shapes=[
            pltpu.VMEM((4, rows, width), jnp.bfloat16),
            pltpu.SemaphoreType.DMA((4, CHUNKS)),
        ],
        compiler_params=pltpu.CompilerParams(vmem_limit_bytes=56 * 2**20),
        name="pack",
    )(queries, keys, values, cross_queries)


def pairs_of(in_ref, slot, write):
    parts, _, rows, _ = in_ref.shape

    @pl.loop(0, parts // 2)
    def _(part):
        where = pl.ds(pl.multiple_of(part * 2 * rows, 16), 2 * rows)
        pieces = [in_ref[2 * part, slot], in_ref[2 * part + 1, slot]]
        write(where, jnp.concatenate(pieces, axis=0))


def unpack_kernel(in_ref, tk_hbm, tv_hbm, q_ref, kv_ref, v_ref, text_ref, sems):
    copies = [
        pltpu.make_async_copy(ref, text_ref.at[side], sems.at[side])
        for side, ref in enumerate((tk_hbm, tv_hbm))
    ]
    for copy in copies:
        copy.start()

    def into(ref):
        def write(where, piece):
            ref[where, :] = piece

        return write

    count = v_ref.shape[0]

    def write_queries(where, piece):
        for place in range(q_ref.shape[0]):
            q_ref[place, where, :] = piece

    pairs_of(in_ref, 0, write_queries)
    pairs_of(in_ref, 1, into(kv_ref.at[0]))
    pairs_of(in_ref, 2, into(v_ref))

    @pl.loop(0, count // HD)
    def _(block):
        where = pl.ds(pl.multiple_of(block * HD, HD), HD)
        kv_ref[1, where, :] = v_ref[where, :].T

    tail = pl.ds(count, text_ref.shape[1])
    for side, copy in enumerate(copies):
        copy.wait()
        kv_ref[side, tail, :] = text_ref[side]


def unpack(received, text_keys, text_values):
    parts, _, rows, width = received.shape
    count = parts * rows
    return pl.pallas_call(
        unpack_kernel,
        in_specs=[VMEM] + [pl.BlockSpec(memory_space=pl.ANY)] * 2,
        out_specs=[VMEM] * 2,
        out_shape=[
            jax.ShapeDtypeStruct((4, count, width), jnp.bfloat16),
            jax.ShapeDtypeStruct((2, count + text_keys.shape[0], width), jnp.bfloat16),
        ],
        scratch_shapes=[
            pltpu.VMEM((count, width), jnp.bfloat16),
            pltpu.VMEM((2,) + text_keys.shape, jnp.bfloat16),
            pltpu.SemaphoreType.DMA((2,)),
        ],
        compiler_params=PARAMS,
        name="unpack",
    )(received, text_keys, text_values)


def unpack_cross_kernel(in_ref, c_hbm, c_ref, sem):
    def write(where, piece):
        c_ref[where, :] = piece

    pairs_of(in_ref, 3, write)
    copy = pltpu.make_async_copy(c_ref, c_hbm, sem)
    copy.start()
    copy.wait()


def unpack_cross(received):
    parts, _, rows, width = received.shape
    count = parts * rows
    return pl.pallas_call(
        unpack_cross_kernel,
        in_specs=[VMEM],
        out_specs=pl.BlockSpec(memory_space=pl.ANY),
        out_shape=jax.ShapeDtypeStruct((count, width), jnp.bfloat16),
        scratch_shapes=[pltpu.VMEM((count, width), jnp.bfloat16), pltpu.SemaphoreType.DMA],
        compiler_params=PARAMS,
        name="unpack_cross",
    )(received)


def scores_of(k, q):
    return lax.dot_general(
        k, q, (((1,), (1,)), ((), ())), preferred_element_type=jnp.float32
    )


def with_ones(v):
    return jnp.concatenate([v, jnp.ones((16, v.shape[1]), v.dtype)], axis=0)


def features_first(v_blocks):
    count = v_blocks.shape[0] // HD
    return jnp.concatenate([v_blocks[i * HD : (i + 1) * HD] for i in range(count)], axis=1)


def key_groups(slot):
    near = across_y1(slot)
    return slot, core_of(slot), near, core_of(near)


def pieces_of(block, count):
    return block[0, pl.ds(0, count), :], with_ones(features_first(block[1, pl.ds(0, count), :]))


def half_of(q_ref, half):
    return q_ref[pl.ds(half * TILE, TILE), :]


def hold(held, blocks):
    @pl.loop(0, held.shape[2] // 32)
    def _(step):
        rows = pl.ds(pl.multiple_of(step * 32, 32), 32)
        for number, block in enumerate(blocks):
            for side in range(2):
                held[number, side, rows, :] = block[side, rows, :]


def mix(place, half, s, v, top_ref, sum_ref):
    p = jnp.exp2((s - top_ref[place, half]) * LOG2).astype(jnp.bfloat16)
    sum_ref[place, half] += jnp.dot(v, p, preferred_element_type=jnp.float32)


def estimate(place, q_ref, keys, top_ref):
    for half in range(q_ref.shape[0] // TILE):
        s = scores_of(keys, half_of(q_ref, half))
        top_ref[place, half] = jnp.max(s, axis=0, keepdims=True)


def add_listed(length, list_ref, held, queries, top_ref, sum_ref, scores):
    count = held.shape[2]
    last = len(scores) - 1

    def item(index):
        code = list_ref[index]
        return code // 4, held.at[code % 4]

    def keys(block):
        return block[0, pl.ds(0, count), :]

    place, block = item(0)
    scores[0][...] = scores_of(keys(block), half_of(queries.at[place], 0))

    @pl.loop(0, length)
    def _(index):
        place, block = item(index)
        k, v = pieces_of(block, count)
        after, block = item(jnp.minimum(index + 1, length - 1))
        for tile in range(last + 1):
            if tile < last:
                scores[tile + 1][...] = scores_of(k, half_of(queries.at[place], tile + 1))
                mix(place, tile, scores[tile][...], v, top_ref, sum_ref)
            else:
                held_scores = scores[last][...]
                scores[0][...] = scores_of(keys(block), half_of(queries.at[after], 0))
                mix(place, tile, held_scores, v, top_ref, sum_ref)


def first_kernel(
    ids_ref, q4_ref, one, two, top_hbm, sum_hbm, held, top_ref, sum_ref, sems, list_ref, *scores
):
    slot = lax.axis_index("group")
    q_ref = q4_ref.at[0]
    hold(held, (one, two))
    sum_ref[...] = jnp.zeros_like(sum_ref)
    estimate(0, q_ref, one[0, pl.ds(0, HD), :], top_ref)
    list_ref[0] = 0
    list_ref[1] = 1
    length = 1 + (ids_ref[core_of(slot)] <= ids_ref[slot]).astype(jnp.int32)
    add_listed(length, list_ref, held, q4_ref, top_ref, sum_ref, scores)
    copies = [
        pltpu.make_async_copy(top_ref, top_hbm, sems.at[0]),
        pltpu.make_async_copy(sum_ref, sum_hbm, sems.at[1]),
    ]
    for copy in copies:
        copy.start()
    for copy in copies:
        copy.wait()


def attend_kernel(
    ids_ref, q_ref, b0, b1, b2, b3, top_hbm, sum_hbm,
    out_ref, queries, held, top_ref, sum_ref, sems, list_ref, full_ref, *scores,
):
    copies = [
        pltpu.make_async_copy(top_hbm.at[0], top_ref.at[0], sems.at[0]),
        pltpu.make_async_copy(sum_hbm.at[0], sum_ref.at[0], sems.at[1]),
    ]
    for copy in copies:
        copy.start()
    slot = lax.axis_index("group")
    blocks = (b0, b1, b2, b3)
    hold(held, blocks)
    count = held.shape[2]
    for step in range(4):
        queries[step] = q_ref[place_across(slot, step)]
    @pl.loop(1, 4)
    def _(place):
        sum_ref[place] = jnp.zeros_like(sum_ref[place])
        estimate(place, queries.at[place], b0[0, pl.ds(0, HD), :], top_ref)

    list_ref[0] = 0
    length = jnp.int32(0)
    full_length = jnp.int32(0)
    seen = []
    for place, owner in enumerate(OWNERS):
        rank = ids_ref[owner(slot)]
        before = full_length
        for number, group in enumerate(key_groups(slot)):
            see = (ids_ref[group] <= rank).astype(jnp.int32)
            full_ref[full_length] = 4 * place + number
            full_length = full_length + see
            if place > 0 or number > 1:
                list_ref[length] = 4 * place + number
                length = length + see
        seen.append(full_length > before)
    for copy in copies:
        copy.wait()
    add_listed(length, list_ref, held, queries, top_ref, sum_ref, scores)

    inside = jnp.bool_(True)
    for place, some in enumerate(seen):
        totals = sum_ref[place, :, HD : HD + 1, :]
        good = (jnp.min(totals) > SMALL) & (jnp.max(totals) < LARGE)
        inside = inside & (good | jnp.logical_not(some))

    @pl.when(jnp.logical_not(inside))
    def _():
        top_ref[...] = jnp.full_like(top_ref, LOW)
        sum_ref[...] = jnp.zeros_like(sum_ref)
        halves = count // TILE

        @pl.loop(0, full_length * halves)
        def _(index):
            code = full_ref[index // halves]
            place, number = code // 4, code % 4
            half = index % halves
            k, v = pieces_of(held.at[number], count)
            where = pl.ds(pl.multiple_of(half * TILE, TILE), TILE)
            s = scores_of(k, queries[place, where, :])
            old = top_ref[place, half]
            new = jnp.maximum(old, jnp.max(s, axis=0, keepdims=True))
            top_ref[place, half] = new
            sum_ref[place, half] = sum_ref[place, half] * jnp.exp2((old - new) * LOG2)
            mix(place, half, s, v, top_ref, sum_ref)

    texts = b0.shape[1] - count
    for number in range(4):
        place = place_across(slot, number)

        @pl.loop(0, count // TILE)
        def _(half):
            def write(start, part):
                where = pl.ds(pl.multiple_of(half * TILE + start, HD), HD)
                out_ref[place, where, :] = part.astype(jnp.bfloat16)

            means(sum_ref[number, half], write)

        logs = log_sums(number, top_ref, sum_ref)
        high = logs.astype(jnp.bfloat16)
        rest = logs - high.astype(jnp.float32)
        mid = rest.astype(jnp.bfloat16)
        low = (rest - mid.astype(jnp.float32)).astype(jnp.bfloat16)
        tail = jnp.concatenate([high, mid, low, jnp.zeros_like(low)], axis=0)
        out_ref[place, pl.ds(count, 32), :] = tail
        for piece in range(8):
            text = blocks[piece // 2][piece % 2, pl.ds(count, texts), :]
            out_ref[place, pl.ds(count + 32 + piece * texts, texts), :] = text


def log_sums(place, top_ref, sum_ref):
    lines = []
    for half in range(top_ref.shape[1]):
        total = sum_ref[place, half, HD : HD + 1, :]
        logs = jnp.where(total > 0, jnp.log2(total) + top_ref[place, half] * LOG2, LOW)
        lines += [logs[:, start : start + HD] for start in range(0, TILE, HD)]
    lines.append(jnp.full((8 - len(lines), HD), LOW, jnp.float32))
    return jnp.concatenate(lines, axis=0)


def means(sums, write):
    for start in range(0, TILE, HD):
        total = sums[HD : HD + 1, start : start + HD]
        write(start, sums[:HD, start : start + HD] / jnp.where(total > 0, total, 1.0))


def cost(parts):
    return pl.CostEstimate(
        flops=parts * 4 * 768 * 768 * 128,
        bytes_accessed=parts * 2**19,
        transcendentals=parts * 768 * 768,
    )


def state(places, count):
    halves = count // TILE
    return [
        jax.ShapeDtypeStruct((places, halves, 1, TILE), jnp.float32),
        jax.ShapeDtypeStruct((places, halves, HD + 16, TILE), jnp.float32),
    ]


def scores_scratch(count):
    return [pltpu.VMEM((count, TILE), jnp.float32)] * (count // TILE)


def first(group_ids, q, one, two):
    count = q.shape[1]
    return pl.pallas_call(
        first_kernel,
        in_specs=[SMEM] + [VMEM] * 3,
        out_specs=[pl.BlockSpec(memory_space=pl.ANY)] * 2,
        out_shape=state(1, count),
        scratch_shapes=[
            pltpu.VMEM((2, 2, count, HD), jnp.bfloat16),
            *(pltpu.VMEM(one.shape, one.dtype) for one in state(1, count)),
            pltpu.SemaphoreType.DMA((2,)),
            pltpu.SMEM((4,), jnp.int32),
            *scores_scratch(count),
        ],
        compiler_params=PARAMS,
        cost_estimate=cost(2),
        name="first",
    )(group_ids, q, one, two)


def attend(group_ids, queries, blocks, begun):
    count = queries.shape[1]
    texts = 8 * (blocks[0].shape[1] - count)
    return pl.pallas_call(
        attend_kernel,
        in_specs=[SMEM] + [VMEM] * 5 + [pl.BlockSpec(memory_space=pl.ANY)] * 2,
        out_specs=VMEM,
        out_shape=jax.ShapeDtypeStruct((4, count + 32 + texts, HD), jnp.bfloat16),
        scratch_shapes=[
            pltpu.VMEM((4, count, HD), jnp.bfloat16),
            pltpu.VMEM((4, 2, count, HD), jnp.bfloat16),
            *(pltpu.VMEM(one.shape, one.dtype) for one in state(4, count)),
            pltpu.SemaphoreType.DMA((2,)),
            pltpu.SMEM((20,), jnp.int32),
            pltpu.SMEM((20,), jnp.int32),
            *scores_scratch(count),
        ],
        compiler_params=PARAMS,
        cost_estimate=cost(12),
        name="attend",
    )(group_ids, queries, *blocks, *begun)


def merge_kernel(
    len_ref, c_hbm, back_ref, gate_hbm, out_ref, c_ref, tk_ref, tv_ref, cross_ref, weight_ref, gate_ref, sems
):
    copy = pltpu.make_async_copy(c_hbm, c_ref, sems.at[0])
    copy.start()
    gate_copy = pltpu.make_async_copy(gate_hbm, gate_ref, sems.at[1])
    gate_copy.start()
    count = c_ref.shape[0]
    pieces, texts, _ = tk_ref.shape
    slot = lax.axis_index("group")
    for step, owner in enumerate(OWNERS):
        ref = back_ref.at[place_across(slot, step)]
        for place, group in enumerate(key_groups(owner(slot))):
            for side, held in enumerate((tk_ref, tv_ref)):
                start = count + 32 + (2 * place + side) * texts
                held[group] = ref[pl.ds(start, texts), :]
    logs = []
    for place in range(4):
        tail = back_ref[place, pl.ds(count, 32), :].astype(jnp.float32)
        logs.append(tail[0:8] + tail[8:16] + tail[16:24])
    best = functools.reduce(jnp.maximum, logs)
    weights = [jnp.exp2(line - best) for line in logs]
    total = functools.reduce(jnp.add, weights)
    for place, weight in enumerate(weights):
        weight_ref[place] = weight / total
    length = pieces * texts
    mask = lax.broadcasted_iota(jnp.int32, (length, 1), 0) < len_ref[0]
    k = tk_ref[...].reshape(length, HD)
    v = with_ones(tv_ref[...].reshape(length, HD).T)
    copy.wait()

    @pl.loop(0, count // TILE)
    def _(half):
        queries = c_ref[pl.ds(pl.multiple_of(half * TILE, TILE), TILE), :]
        s = jnp.where(mask, scores_of(k, queries), LOW)
        top = jnp.max(s, axis=0, keepdims=True)
        p = jnp.exp2((s - top) * LOG2).astype(jnp.bfloat16)
        sums = jnp.dot(v, p, preferred_element_type=jnp.float32)

        def write(start, part):
            cross_ref[pl.ds(pl.multiple_of(half * TILE + start, HD), HD), :] = part

        means(sums, write)

    gate_copy.wait()
    gate = jnp.broadcast_to(gate_ref[...], (HD, HD)).T

    @pl.loop(0, count // HD)
    def _(step):
        rows = pl.ds(pl.multiple_of(step * HD, HD), HD)
        mixed = None
        for place in range(4):
            line = weight_ref[place, pl.ds(step, 1), :]
            part = line * back_ref[place, rows, :].astype(jnp.float32)
            mixed = part if mixed is None else mixed + part
        out_ref[rows, :] = (gate * mixed + cross_ref[rows, :]).astype(jnp.bfloat16).T


def merge(text_len, cross, back, gate):
    anywhere = pl.BlockSpec(memory_space=pl.ANY)
    count = cross.shape[0]
    held = pltpu.VMEM((16, (back.shape[1] - count - 32) // 8, HD), jnp.bfloat16)
    return pl.pallas_call(
        merge_kernel,
        in_specs=[SMEM, anywhere, VMEM, anywhere],
        out_specs=VMEM,
        out_shape=jax.ShapeDtypeStruct((count, HD), jnp.bfloat16),
        scratch_shapes=[
            pltpu.VMEM((count, HD), jnp.bfloat16),
            held,
            held,
            pltpu.VMEM((count, HD), jnp.float32),
            pltpu.VMEM((4, 8, HD), jnp.float32),
            pltpu.VMEM(gate.shape, jnp.float32),
            pltpu.SemaphoreType.DMA((2,)),
        ],
        compiler_params=PARAMS,
        cost_estimate=cost(1),
        name="merge",
    )(text_len, cross, back, gate)


def to_heads(array):
    return lax.all_to_all(array, "seq", split_axis=0, concat_axis=0, tiled=True)


def body(
    queries, keys, values, cross_queries, text_keys, text_values, group_gate, group_ids, text_len
):
    packed = pack(queries, keys, values, cross_queries)
    received = to_heads(packed)
    q, kv = unpack(received, text_keys, text_values)
    cross = unpack_cross(received)
    kv_core = swap(kv, core_of)
    kv_near = swap(kv, across_y1)
    begun = first(group_ids, q, kv, kv_core)
    q, kv_core = lax.optimization_barrier((q, kv_core))
    blocks = (kv, kv_core, kv_near, swap(kv_near, core_of))
    back = in_cluster(attend(group_ids, in_cluster(q), blocks, begun))
    mixed = merge(text_len, cross, back, group_gate)
    count = mixed.shape[0]
    heads = lax.axis_size("seq")
    mixed = to_heads(mixed.reshape(heads, count // heads, HD))
    return jnp.transpose(mixed, (1, 0, 2)).reshape(1, count // heads, heads * HD)


def solution(mesh):
    return jax.shard_map(
        body,
        mesh=mesh,
        in_specs=(
            P("group", "seq", None),
            P("group", "seq", None),
            P("group", "seq", None),
            P("group", "seq", None),
            P("group", "seq"),
            P("group", "seq"),
            P("group", "seq"),
            P(),
            P(),
        ),
        out_specs=P("group", "seq", None),
        check_vma=False,
    )
```

```python
import functools
import math

import jax
import jax.numpy as jnp
from jax import lax
from jax.experimental import pallas as pl
from jax.experimental.pallas import tpu as pltpu
from jax.sharding import PartitionSpec as P

HD = 128
LOG2 = math.log2(math.e) / math.sqrt(HD)
LOW = -1e30
VMEM = pl.BlockSpec(memory_space=pltpu.VMEM)
SMEM = pl.BlockSpec(memory_space=pltpu.SMEM)
HBM = pl.BlockSpec(memory_space=pltpu.HBM)
PARAMS = pltpu.CompilerParams(vmem_limit_bytes=14 * 2**20)


SMALL, LARGE = 2.0**-60, 2.0**90
TILE = 384


def core_of(i):
    return i + 1 - 2 * (i % 2)


def across_x(i):
    return (i + 8) % 16


def across_y1(i):
    y = (i // 2) % 4
    return i + 2 * (1 - 2 * (y % 2))


def across_y2(i):
    y = (i // 2) % 4
    return (i // 8) * 8 + ((y + 2 * (y % 2) + 3) % 4) * 2 + i % 2


def across_xy2(i):
    return across_x(across_y2(i))


CLUSTERS = [
    [i, across_x(i), across_y2(i), across_xy2(i)] for i in (2, 3, 6, 7)
]
OWNERS = (lambda i: i, across_x, across_y2, across_xy2)


def place_of(i):
    y = (i // 2) % 4
    return i // 8 + 2 * ((y + 1) % 2)


def place_across(i, step):
    place = place_of(i)
    x, y = place % 2, place // 2
    if step % 2:
        x = 1 - x
    if step // 2:
        y = 1 - y
    return x + 2 * y


def in_cluster(array):
    return lax.all_to_all(
        array, "group", split_axis=0, concat_axis=0, axis_index_groups=CLUSTERS, tiled=True
    )


def swap(array, partner):
    return lax.ppermute(array, "group", [(i, partner(i)) for i in range(16)])


CHUNKS = 4


def pack_kernel(q_hbm, k_hbm, v_hbm, c_hbm, out_ref, held, sems):
    sources = (q_hbm, k_hbm, v_hbm, c_hbm)
    heads = out_ref.shape[0]
    chunk = heads // CHUNKS * HD
    copies = []
    for slot, ref in enumerate(sources):
        for part in range(CHUNKS):
            where = pl.ds(part * chunk, chunk)
            copy = pltpu.make_async_copy(
                ref.at[0, :, where], held.at[slot, :, where], sems.at[slot, part]
            )
            copy.start()
            copies.append(copy)
    for slot in range(len(sources)):
        for part in range(CHUNKS):
            copies[slot * CHUNKS + part].wait()
            for head in range(part * heads // CHUNKS, (part + 1) * heads // CHUNKS):
                out_ref[head, slot] = held[slot, :, head * HD : (head + 1) * HD]


def pack(queries, keys, values, cross_queries):
    rows, width = queries.shape[1:]
    heads = width // HD
    return pl.pallas_call(
        pack_kernel,
        in_specs=[pl.BlockSpec(memory_space=pl.ANY)] * 4,
        out_specs=VMEM,
        out_shape=jax.ShapeDtypeStruct((heads, 4, rows, HD), jnp.bfloat16),
        scratch_shapes=[
            pltpu.VMEM((4, rows, width), jnp.bfloat16),
            pltpu.SemaphoreType.DMA((4, CHUNKS)),
        ],
        compiler_params=pltpu.CompilerParams(vmem_limit_bytes=56 * 2**20),
        name="pack",
    )(queries, keys, values, cross_queries)


def pairs_of(in_ref, slot, write):
    parts, _, rows, _ = in_ref.shape

    @pl.loop(0, parts // 2)
    def _(part):
        where = pl.ds(pl.multiple_of(part * 2 * rows, 16), 2 * rows)
        pieces = [in_ref[2 * part, slot], in_ref[2 * part + 1, slot]]
        write(where, jnp.concatenate(pieces, axis=0))


def unpack_kernel(in_ref, tk_hbm, tv_hbm, q_ref, kv_ref, all_ref, v_ref, text_ref, sems):
    copies = [
        pltpu.make_async_copy(ref, text_ref.at[side], sems.at[side])
        for side, ref in enumerate((tk_hbm, tv_hbm))
    ]
    for copy in copies:
        copy.start()

    def into(ref):
        def write(where, piece):
            ref[where, :] = piece

        return write

    count = v_ref.shape[0]

    def write_queries(where, piece):
        for place in range(q_ref.shape[0]):
            q_ref[place, where, :] = piece

    pairs_of(in_ref, 0, write_queries)
    pairs_of(in_ref, 1, into(kv_ref.at[0]))
    pairs_of(in_ref, 2, into(v_ref))

    @pl.loop(0, count // HD)
    def _(block):
        where = pl.ds(pl.multiple_of(block * HD, HD), HD)
        kv_ref[1, where, :] = v_ref[where, :].T

    for copy in copies:
        copy.wait()
    for place in range(all_ref.shape[0]):
        all_ref[place] = text_ref[...]


def unpack(received, text_keys, text_values):
    parts, _, rows, width = received.shape
    count = parts * rows
    return pl.pallas_call(
        unpack_kernel,
        in_specs=[VMEM] + [HBM] * 2,
        out_specs=[VMEM] * 3,
        out_shape=[
            jax.ShapeDtypeStruct((4, count, width), jnp.bfloat16),
            jax.ShapeDtypeStruct((2, count, width), jnp.bfloat16),
            jax.ShapeDtypeStruct((16, 2) + text_keys.shape, jnp.bfloat16),
        ],
        scratch_shapes=[
            pltpu.VMEM((count, width), jnp.bfloat16),
            pltpu.VMEM((2,) + text_keys.shape, jnp.bfloat16),
            pltpu.SemaphoreType.DMA((2,)),
        ],
        compiler_params=PARAMS,
        name="unpack",
    )(received, text_keys, text_values)


def scores_of(k, q):
    return lax.dot_general(
        k, q, (((1,), (1,)), ((), ())), preferred_element_type=jnp.float32
    )


def with_ones(v):
    return jnp.concatenate([v, jnp.ones((16, v.shape[1]), v.dtype)], axis=0)


def features_first(v_blocks):
    count = v_blocks.shape[0] // HD
    return jnp.concatenate([v_blocks[i * HD : (i + 1) * HD] for i in range(count)], axis=1)


def key_groups(slot):
    near = across_y1(slot)
    return slot, core_of(slot), near, core_of(near)


def pieces_of(block, count):
    return block[0, pl.ds(0, count), :], with_ones(features_first(block[1, pl.ds(0, count), :]))


def half_of(q_ref, half):
    return q_ref[pl.ds(half * TILE, TILE), :]


def hold(held, blocks):
    @pl.loop(0, held.shape[2] // 32)
    def _(step):
        rows = pl.ds(pl.multiple_of(step * 32, 32), 32)
        for number, block in enumerate(blocks):
            for side in range(2):
                held[number, side, rows, :] = block[side, rows, :]


def mix(place, half, s, v, top_ref, sum_ref):
    p = jnp.exp2((s - top_ref[place, half]) * LOG2).astype(jnp.bfloat16)
    sum_ref[place, half] += jnp.dot(v, p, preferred_element_type=jnp.float32)


def estimate(place, q_ref, keys, top_ref):
    for half in range(q_ref.shape[0] // TILE):
        s = scores_of(keys, half_of(q_ref, half))
        top_ref[place, half] = jnp.max(s, axis=0, keepdims=True)


def add_listed(length, list_ref, held, queries, top_ref, sum_ref, scores):
    count = held.shape[2]
    last = len(scores) - 1

    def item(index):
        code = list_ref[index]
        return code // 4, held.at[code % 4]

    def keys(block):
        return block[0, pl.ds(0, count), :]

    place, block = item(0)
    scores[0][...] = scores_of(keys(block), half_of(queries.at[place], 0))

    @pl.loop(0, length)
    def _(index):
        place, block = item(index)
        k, v = pieces_of(block, count)
        after, block = item(jnp.minimum(index + 1, length - 1))
        for tile in range(last + 1):
            if tile < last:
                scores[tile + 1][...] = scores_of(k, half_of(queries.at[place], tile + 1))
                mix(place, tile, scores[tile][...], v, top_ref, sum_ref)
            else:
                held_scores = scores[last][...]
                scores[0][...] = scores_of(keys(block), half_of(queries.at[after], 0))
                mix(place, tile, held_scores, v, top_ref, sum_ref)


def first_kernel(
    ids_ref, q4_ref, one, two, top_hbm, sum_hbm, held, top_ref, sum_ref, sems, list_ref, *scores
):
    slot = lax.axis_index("group")
    q_ref = q4_ref.at[0]
    hold(held, (one, two))
    sum_ref[...] = jnp.zeros_like(sum_ref)
    estimate(0, q_ref, one[0, pl.ds(0, HD), :], top_ref)
    list_ref[0] = 0
    list_ref[1] = 1
    length = 1 + (ids_ref[core_of(slot)] <= ids_ref[slot]).astype(jnp.int32)
    add_listed(length, list_ref, held, q4_ref, top_ref, sum_ref, scores)
    copies = [
        pltpu.make_async_copy(top_ref, top_hbm, sems.at[0]),
        pltpu.make_async_copy(sum_ref, sum_hbm, sems.at[1]),
    ]
    for copy in copies:
        copy.start()
    for copy in copies:
        copy.wait()


def attend_to(
    steps, begun, ids_ref, q_ref, blocks, queries, held, top_ref, sum_ref, list_ref, full_ref, scores
):
    slot = lax.axis_index("group")
    hold(held, blocks)
    count = held.shape[2]
    for number, step in enumerate(steps):
        queries[number] = q_ref[place_across(slot, step)]

    if not begun:

        @pl.loop(0, len(steps))
        def _(number):
            sum_ref[number] = jnp.zeros_like(sum_ref[number])
            estimate(number, queries.at[number], blocks[0][0, pl.ds(0, HD), :], top_ref)

    list_ref[0] = 0
    length = jnp.int32(0)
    full_length = jnp.int32(0)
    seen = []
    for number, step in enumerate(steps):
        rank = ids_ref[OWNERS[step](slot)]
        before = full_length
        for block, group in enumerate(key_groups(slot)):
            see = (ids_ref[group] <= rank).astype(jnp.int32)
            full_ref[full_length] = 4 * number + block
            full_length = full_length + see
            if block > 1 or not begun:
                list_ref[length] = 4 * number + block
                length = length + see
        seen.append(full_length > before)
    if begun:
        for copy in begun:
            copy.wait()
    add_listed(length, list_ref, held, queries, top_ref, sum_ref, scores)

    inside = jnp.bool_(True)
    for number, some in enumerate(seen):
        totals = sum_ref[number, :, HD : HD + 1, :]
        good = (jnp.min(totals) > SMALL) & (jnp.max(totals) < LARGE)
        inside = inside & (good | jnp.logical_not(some))

    @pl.when(jnp.logical_not(inside))
    def _():
        top_ref[...] = jnp.full_like(top_ref, LOW)
        sum_ref[...] = jnp.zeros_like(sum_ref)
        halves = count // TILE

        @pl.loop(0, full_length * halves)
        def _(index):
            code = full_ref[index // halves]
            number, block = code // 4, code % 4
            half = index % halves
            k, v = pieces_of(held.at[block], count)
            where = pl.ds(pl.multiple_of(half * TILE, TILE), TILE)
            s = scores_of(k, queries[number, where, :])
            old = top_ref[number, half]
            new = jnp.maximum(old, jnp.max(s, axis=0, keepdims=True))
            top_ref[number, half] = new
            sum_ref[number, half] = sum_ref[number, half] * jnp.exp2((old - new) * LOG2)
            mix(number, half, s, v, top_ref, sum_ref)


def attend_kernel(
    ids_ref, q_ref, b0, b1, b2, b3,
    out_ref, queries, held, top_ref, sum_ref, list_ref, full_ref, *scores,
):
    attend_to(
        (1, 2, 3), (), ids_ref, q_ref, (b0, b1, b2, b3),
        queries, held, top_ref, sum_ref, list_ref, full_ref, scores,
    )
    slot = lax.axis_index("group")
    count = held.shape[2]
    for number in range(3):
        place = place_across(slot, number + 1)

        @pl.loop(0, count // TILE)
        def _(half):
            def write(start, part):
                where = pl.ds(pl.multiple_of(half * TILE + start, HD), HD)
                out_ref[place, where, :] = part.astype(jnp.bfloat16)

            means(sum_ref[number, half], write)

        logs = log_sums(number, top_ref, sum_ref)
        high = logs.astype(jnp.bfloat16)
        rest = logs - high.astype(jnp.float32)
        mid = rest.astype(jnp.bfloat16)
        low = (rest - mid.astype(jnp.float32)).astype(jnp.bfloat16)
        tail = jnp.concatenate([high, mid, low, jnp.zeros_like(low)], axis=0)
        out_ref[place, pl.ds(count, 32), :] = tail


def own_kernel(
    ids_ref, q_ref, b0, b1, b2, b3, top_hbm, sum_hbm,
    out_ref, queries, held, top_ref, sum_ref, sems, list_ref, full_ref, *scores,
):
    copies = [
        pltpu.make_async_copy(top_hbm, top_ref, sems.at[0]),
        pltpu.make_async_copy(sum_hbm, sum_ref, sems.at[1]),
    ]
    for copy in copies:
        copy.start()
    attend_to(
        (0,), copies, ids_ref, q_ref, (b0, b1, b2, b3),
        queries, held, top_ref, sum_ref, list_ref, full_ref, scores,
    )
    count = held.shape[2]

    @pl.loop(0, count // TILE)
    def _(half):
        def write(start, part):
            out_ref[pl.ds(pl.multiple_of(half * TILE + start, HD), HD), :] = part

        means(sum_ref[0, half], write)

    out_ref[pl.ds(count, 8), :] = log_sums(0, top_ref, sum_ref)


def log_sums(place, top_ref, sum_ref):
    lines = []
    for half in range(top_ref.shape[1]):
        total = sum_ref[place, half, HD : HD + 1, :]
        logs = jnp.where(total > 0, jnp.log2(total) + top_ref[place, half] * LOG2, LOW)
        lines += [logs[:, start : start + HD] for start in range(0, TILE, HD)]
    lines.append(jnp.full((8 - len(lines), HD), LOW, jnp.float32))
    return jnp.concatenate(lines, axis=0)


def means(sums, write):
    for start in range(0, TILE, HD):
        total = sums[HD : HD + 1, start : start + HD]
        write(start, sums[:HD, start : start + HD] / jnp.where(total > 0, total, 1.0))


def cost(parts):
    return pl.CostEstimate(
        flops=parts * 4 * 768 * 768 * 128,
        bytes_accessed=parts * 2**19,
        transcendentals=parts * 768 * 768,
    )


def state(places, count):
    halves = count // TILE
    return [
        jax.ShapeDtypeStruct((places, halves, 1, TILE), jnp.float32),
        jax.ShapeDtypeStruct((places, halves, HD + 16, TILE), jnp.float32),
    ]


def scores_scratch(count):
    return [pltpu.VMEM((count, TILE), jnp.float32)] * (count // TILE)


def first(group_ids, q, one, two):
    count = q.shape[1]
    return pl.pallas_call(
        first_kernel,
        in_specs=[SMEM] + [VMEM] * 3,
        out_specs=[HBM] * 2,
        out_shape=state(1, count),
        scratch_shapes=[
            pltpu.VMEM((2, 2, count, HD), jnp.bfloat16),
            *(pltpu.VMEM(one.shape, one.dtype) for one in state(1, count)),
            pltpu.SemaphoreType.DMA((2,)),
            pltpu.SMEM((4,), jnp.int32),
            *scores_scratch(count),
        ],
        compiler_params=PARAMS,
        cost_estimate=cost(2),
        name="first",
    )(group_ids, q, one, two)


def attend_scratch(places, count):
    return [
        pltpu.VMEM((places, count, HD), jnp.bfloat16),
        pltpu.VMEM((4, 2, count, HD), jnp.bfloat16),
        *(pltpu.VMEM(one.shape, one.dtype) for one in state(places, count)),
    ]


def lists(places):
    return [pltpu.SMEM((4 * places + 4,), jnp.int32)] * 2


def attend(group_ids, queries, blocks):
    count = queries.shape[1]
    return pl.pallas_call(
        attend_kernel,
        in_specs=[SMEM] + [VMEM] * 5,
        out_specs=VMEM,
        out_shape=jax.ShapeDtypeStruct((4, count + 32, HD), jnp.bfloat16),
        scratch_shapes=[*attend_scratch(3, count), *lists(3), *scores_scratch(count)],
        compiler_params=PARAMS,
        cost_estimate=cost(12),
        name="attend",
    )(group_ids, queries, *blocks)


def own(group_ids, queries, blocks, begun):
    count = queries.shape[1]
    return pl.pallas_call(
        own_kernel,
        in_specs=[SMEM] + [VMEM] * 5 + [HBM] * 2,
        out_specs=VMEM,
        out_shape=jax.ShapeDtypeStruct((count + 8, HD), jnp.float32),
        scratch_shapes=[
            *attend_scratch(1, count),
            pltpu.SemaphoreType.DMA((2,)),
            *lists(1),
            *scores_scratch(count),
        ],
        compiler_params=PARAMS,
        cost_estimate=cost(2),
        name="own",
    )(group_ids, queries, *blocks, *begun)


def cross_kernel(len_ref, in_ref, text_ref, out_hbm, c_ref, cross_ref, sem):
    def write_queries(where, piece):
        c_ref[where, :] = piece

    pairs_of(in_ref, 3, write_queries)
    pieces, _, texts, _ = text_ref.shape
    length = pieces * texts
    mask = lax.broadcasted_iota(jnp.int32, (length, 1), 0) < len_ref[0]
    k = text_ref[:, 0].reshape(length, HD)
    v = with_ones(text_ref[:, 1].reshape(length, HD).T)

    @pl.loop(0, c_ref.shape[0] // TILE)
    def _(half):
        queries = c_ref[pl.ds(pl.multiple_of(half * TILE, TILE), TILE), :]
        s = jnp.where(mask, scores_of(k, queries), LOW)
        top = jnp.max(s, axis=0, keepdims=True)
        p = jnp.exp2((s - top) * LOG2).astype(jnp.bfloat16)
        sums = jnp.dot(v, p, preferred_element_type=jnp.float32)

        def write(start, part):
            cross_ref[pl.ds(pl.multiple_of(half * TILE + start, HD), HD), :] = part

        means(sums, write)

    copy = pltpu.make_async_copy(cross_ref, out_hbm, sem)
    copy.start()
    copy.wait()


def cross_part(text_len, received, text):
    parts, _, rows, width = received.shape
    count = parts * rows
    return pl.pallas_call(
        cross_kernel,
        in_specs=[SMEM] + [VMEM] * 2,
        out_specs=HBM,
        out_shape=jax.ShapeDtypeStruct((count, width), jnp.float32),
        scratch_shapes=[
            pltpu.VMEM((count, width), jnp.bfloat16),
            pltpu.VMEM((count, width), jnp.float32),
            pltpu.SemaphoreType.DMA,
        ],
        compiler_params=PARAMS,
        cost_estimate=cost(2),
        name="cross",
    )(text_len, received, text)


def merge_kernel(
    own_hbm, cross_hbm, back_ref, gate_hbm, out_ref, own_ref, cross_ref, weight_ref, gate_ref, sems
):
    copies = [
        pltpu.make_async_copy(source, target, sems.at[number])
        for number, (source, target) in enumerate(
            ((own_hbm, own_ref), (cross_hbm, cross_ref), (gate_hbm, gate_ref))
        )
    ]
    for copy in copies:
        copy.start()
    slot = lax.axis_index("group")
    count = cross_ref.shape[0]
    received = [back_ref.at[place_across(slot, step)] for step in (1, 2, 3)]
    logs = []
    for ref in received:
        tail = ref[pl.ds(count, 32), :].astype(jnp.float32)
        logs.append(tail[0:8] + tail[8:16] + tail[16:24])
    for copy in copies:
        copy.wait()
    logs.append(own_ref[pl.ds(count, 8), :])
    best = functools.reduce(jnp.maximum, logs)
    weights = [jnp.exp2(line - best) for line in logs]
    total = functools.reduce(jnp.add, weights)
    for place, weight in enumerate(weights):
        weight_ref[place] = weight / total
    gate = jnp.broadcast_to(gate_ref[...], (HD, HD)).T

    @pl.loop(0, count // HD)
    def _(step):
        rows = pl.ds(pl.multiple_of(step * HD, HD), HD)
        mixed = weight_ref[3, pl.ds(step, 1), :] * own_ref[rows, :]
        for place, ref in enumerate(received):
            line = weight_ref[place, pl.ds(step, 1), :]
            mixed = mixed + line * ref[rows, :].astype(jnp.float32)
        out_ref[rows, :] = (gate * mixed + cross_ref[rows, :]).astype(jnp.bfloat16).T


def merge(mine, cross, back, gate):
    return pl.pallas_call(
        merge_kernel,
        in_specs=[HBM, HBM, VMEM, HBM],
        out_specs=VMEM,
        out_shape=jax.ShapeDtypeStruct(cross.shape, jnp.bfloat16),
        scratch_shapes=[
            pltpu.VMEM(mine.shape, jnp.float32),
            pltpu.VMEM(cross.shape, jnp.float32),
            pltpu.VMEM((4, 8, HD), jnp.float32),
            pltpu.VMEM(gate.shape, jnp.float32),
            pltpu.SemaphoreType.DMA((3,)),
        ],
        compiler_params=PARAMS,
        cost_estimate=cost(1),
        name="merge",
    )(mine, cross, back, gate)


def to_heads(array):
    return lax.all_to_all(array, "seq", split_axis=0, concat_axis=0, tiled=True)


def body(
    queries, keys, values, cross_queries, text_keys, text_values, group_gate, group_ids, text_len
):
    packed = pack(queries, keys, values, cross_queries)
    received = to_heads(packed)
    q, kv, text = unpack(received, text_keys, text_values)
    kv_core = swap(kv, core_of)
    kv_near = swap(kv, across_y1)
    begun = first(group_ids, q, kv, kv_core)
    q, kv_core = lax.optimization_barrier((q, kv_core))
    text, begun = lax.optimization_barrier((text, begun))
    text = lax.all_to_all(text, "group", split_axis=0, concat_axis=0, tiled=True)
    blocks = (kv, kv_core, kv_near, swap(kv_near, core_of))
    q = in_cluster(q)
    sent, q, text = lax.optimization_barrier((attend(group_ids, q, blocks), q, text))
    back = in_cluster(sent)
    mine = own(group_ids, q, blocks, begun)
    mixed = merge(mine, cross_part(text_len, received, text), back, group_gate)
    count = mixed.shape[0]
    heads = lax.axis_size("seq")
    mixed = to_heads(mixed.reshape(heads, count // heads, HD))
    return jnp.transpose(mixed, (1, 0, 2)).reshape(1, count // heads, heads * HD)


def solution(mesh):
    return jax.shard_map(
        body,
        mesh=mesh,
        in_specs=(
            P("group", "seq", None),
            P("group", "seq", None),
            P("group", "seq", None),
            P("group", "seq", None),
            P("group", "seq"),
            P("group", "seq"),
            P("group", "seq"),
            P(),
            P(),
        ),
        out_specs=P("group", "seq", None),
        check_vma=False,
    )
```

```python
import functools
import math

import jax
import jax.numpy as jnp
from jax import lax
from jax.experimental import pallas as pl
from jax.experimental.pallas import tpu as pltpu
from jax.sharding import PartitionSpec as P

HD = 128
LOG2 = math.log2(math.e) / math.sqrt(HD)
LOW = -1e30
VMEM = pl.BlockSpec(memory_space=pltpu.VMEM)
SMEM = pl.BlockSpec(memory_space=pltpu.SMEM)
HBM = pl.BlockSpec(memory_space=pltpu.HBM)
PARAMS = pltpu.CompilerParams(vmem_limit_bytes=14 * 2**20)


SMALL, LARGE = 2.0**-60, 2.0**90
TILE = 384


def core_of(i):
    return i + 1 - 2 * (i % 2)


def across_x(i):
    return (i + 8) % 16


def across_y1(i):
    y = (i // 2) % 4
    return i + 2 * (1 - 2 * (y % 2))


def across_y2(i):
    y = (i // 2) % 4
    return (i // 8) * 8 + ((y + 2 * (y % 2) + 3) % 4) * 2 + i % 2


def across_xy2(i):
    return across_x(across_y2(i))


CLUSTERS = [
    [i, across_x(i), across_y2(i), across_xy2(i)] for i in (2, 3, 6, 7)
]
OWNERS = (lambda i: i, across_x, across_y2, across_xy2)


def place_of(i):
    y = (i // 2) % 4
    return i // 8 + 2 * ((y + 1) % 2)


def place_across(i, step):
    place = place_of(i)
    x, y = place % 2, place // 2
    if step % 2:
        x = 1 - x
    if step // 2:
        y = 1 - y
    return x + 2 * y


def in_cluster(array):
    return lax.all_to_all(
        array, "group", split_axis=0, concat_axis=0, axis_index_groups=CLUSTERS, tiled=True
    )


def swap(array, partner):
    return lax.ppermute(array, "group", [(i, partner(i)) for i in range(16)])


CHUNKS = 4


def pack_kernel(q_hbm, k_hbm, v_hbm, c_hbm, out_ref, held, sems):
    sources = (q_hbm, k_hbm, v_hbm, c_hbm)
    heads = out_ref.shape[0]
    chunk = heads // CHUNKS * HD
    copies = []
    for slot, ref in enumerate(sources):
        for part in range(CHUNKS):
            where = pl.ds(part * chunk, chunk)
            copy = pltpu.make_async_copy(
                ref.at[0, :, where], held.at[slot, :, where], sems.at[slot, part]
            )
            copy.start()
            copies.append(copy)
    for slot in range(len(sources)):
        for part in range(CHUNKS):
            copies[slot * CHUNKS + part].wait()
            for head in range(part * heads // CHUNKS, (part + 1) * heads // CHUNKS):
                out_ref[head, slot] = held[slot, :, head * HD : (head + 1) * HD]


def pack(queries, keys, values, cross_queries):
    rows, width = queries.shape[1:]
    heads = width // HD
    return pl.pallas_call(
        pack_kernel,
        in_specs=[pl.BlockSpec(memory_space=pl.ANY)] * 4,
        out_specs=VMEM,
        out_shape=jax.ShapeDtypeStruct((heads, 4, rows, HD), jnp.bfloat16),
        scratch_shapes=[
            pltpu.VMEM((4, rows, width), jnp.bfloat16),
            pltpu.SemaphoreType.DMA((4, CHUNKS)),
        ],
        compiler_params=pltpu.CompilerParams(vmem_limit_bytes=56 * 2**20),
        name="pack",
    )(queries, keys, values, cross_queries)


def pairs_of(in_ref, slot, write):
    parts, _, rows, _ = in_ref.shape

    @pl.loop(0, parts // 2)
    def _(part):
        where = pl.ds(pl.multiple_of(part * 2 * rows, 16), 2 * rows)
        pieces = [in_ref[2 * part, slot], in_ref[2 * part + 1, slot]]
        write(where, jnp.concatenate(pieces, axis=0))


def unpack_kernel(in_ref, tk_hbm, tv_hbm, q_ref, kv_ref, all_ref, v_ref, text_ref, sems):
    copies = [
        pltpu.make_async_copy(ref, text_ref.at[side], sems.at[side])
        for side, ref in enumerate((tk_hbm, tv_hbm))
    ]
    for copy in copies:
        copy.start()

    def into(ref):
        def write(where, piece):
            ref[where, :] = piece

        return write

    count = v_ref.shape[0]

    def write_queries(where, piece):
        for place in range(q_ref.shape[0]):
            q_ref[place, where, :] = piece

    pairs_of(in_ref, 0, write_queries)
    pairs_of(in_ref, 1, into(kv_ref.at[0]))
    pairs_of(in_ref, 2, into(v_ref))

    @pl.loop(0, count // HD)
    def _(block):
        where = pl.ds(pl.multiple_of(block * HD, HD), HD)
        kv_ref[1, where, :] = v_ref[where, :].T

    for copy in copies:
        copy.wait()
    for place in range(all_ref.shape[0]):
        all_ref[place] = text_ref[...]


def unpack(received, text_keys, text_values):
    parts, _, rows, width = received.shape
    count = parts * rows
    return pl.pallas_call(
        unpack_kernel,
        in_specs=[VMEM] + [HBM] * 2,
        out_specs=[VMEM] * 3,
        out_shape=[
            jax.ShapeDtypeStruct((4, count, width), jnp.bfloat16),
            jax.ShapeDtypeStruct((2, count, width), jnp.bfloat16),
            jax.ShapeDtypeStruct((16, 2) + text_keys.shape, jnp.bfloat16),
        ],
        scratch_shapes=[
            pltpu.VMEM((count, width), jnp.bfloat16),
            pltpu.VMEM((2,) + text_keys.shape, jnp.bfloat16),
            pltpu.SemaphoreType.DMA((2,)),
        ],
        compiler_params=PARAMS,
        name="unpack",
    )(received, text_keys, text_values)


def scores_of(k, q):
    return lax.dot_general(
        k, q, (((1,), (1,)), ((), ())), preferred_element_type=jnp.float32
    )


def with_ones(v):
    return jnp.concatenate([v, jnp.ones((16, v.shape[1]), v.dtype)], axis=0)


def features_first(v_blocks):
    count = v_blocks.shape[0] // HD
    return jnp.concatenate([v_blocks[i * HD : (i + 1) * HD] for i in range(count)], axis=1)


def key_groups(slot):
    near = across_y1(slot)
    return slot, core_of(slot), near, core_of(near)


def keys_of(blocks, count):
    return jnp.concatenate([block[0, pl.ds(0, count), :] for block in blocks], axis=0)


def values_of(blocks, count):
    parts = [features_first(block[1, pl.ds(0, count), :]) for block in blocks]
    return with_ones(jnp.concatenate(parts, axis=1))


def half_of(q_ref, half):
    return q_ref[pl.ds(half * TILE, TILE), :]


def hold(held, blocks):
    @pl.loop(0, held.shape[2] // 32)
    def _(step):
        rows = pl.ds(pl.multiple_of(step * 32, 32), 32)
        for number, block in enumerate(blocks):
            for side in range(2):
                held[number, side, rows, :] = block[side, rows, :]


def mix(place, half, s, v, top_ref, sum_ref):
    p = jnp.exp2((s - top_ref[place, half]) * LOG2).astype(jnp.bfloat16)
    sum_ref[place, half] += jnp.dot(v, p, preferred_element_type=jnp.float32)


def estimate(place, q_ref, keys, top_ref):
    for half in range(q_ref.shape[0] // TILE):
        s = scores_of(keys, half_of(q_ref, half))
        top_ref[place, half] = jnp.max(s, axis=0, keepdims=True)


def add_listed(length, list_ref, width, held, queries, top_ref, sum_ref, scores):
    count = held.shape[2]
    last = len(scores) - 1
    scores = [ref.at[pl.ds(0, width * count), :] for ref in scores]

    def item(index):
        code = list_ref[index]
        blocks = [held.at[code // 4**digit % 4] for digit in range(width)]
        return code // 4**width, blocks

    @pl.when(length > 0)
    def _():
        place, blocks = item(0)
        scores[0][...] = scores_of(keys_of(blocks, count), half_of(queries.at[place], 0))

        @pl.loop(0, length)
        def _(index):
            place, blocks = item(index)
            k, v = keys_of(blocks, count), values_of(blocks, count)
            after, blocks = item(jnp.minimum(index + 1, length - 1))
            for tile in range(last):
                scores[tile + 1][...] = scores_of(k, half_of(queries.at[place], tile + 1))
                mix(place, tile, scores[tile][...], v, top_ref, sum_ref)
            final = scores[last][...]
            scores[0][...] = scores_of(keys_of(blocks, count), half_of(queries.at[after], 0))
            mix(place, last, final, v, top_ref, sum_ref)


def add_seen(sees, held, queries, top_ref, sum_ref, pair_ref, one_ref, scores):
    pairs, ones = jnp.int32(0), jnp.int32(0)
    for place, row in enumerate(sees):
        waiting, waits = jnp.int32(0), jnp.int32(0)
        for block, see in row:
            pair_ref[pairs] = 16 * place + 4 * waiting + block
            pairs = pairs + see * waits
            waiting = jnp.where(waits > 0, waiting, block)
            waits = (waits + see) % 2
            waiting = jnp.where(waits > 0, waiting, 0)
        one_ref[ones] = 4 * place + waiting
        ones = ones + waits
    add_listed(pairs, pair_ref, 2, held, queries, top_ref, sum_ref, scores)
    add_listed(ones, one_ref, 1, held, queries, top_ref, sum_ref, scores)


def first_kernel(
    ids_ref, q4_ref, one, two, top_hbm, sum_hbm, held, top_ref, sum_ref, sems, pair_ref, one_ref, *scores
):
    slot = lax.axis_index("group")
    q_ref = q4_ref.at[0]
    hold(held, (one, two))
    sum_ref[...] = jnp.zeros_like(sum_ref)
    estimate(0, q_ref, one[0, pl.ds(0, HD), :], top_ref)
    see = (ids_ref[core_of(slot)] <= ids_ref[slot]).astype(jnp.int32)
    sees = [[(0, jnp.int32(1)), (1, see)]]
    add_seen(sees, held, q4_ref, top_ref, sum_ref, pair_ref, one_ref, scores)
    copies = [
        pltpu.make_async_copy(top_ref, top_hbm, sems.at[0]),
        pltpu.make_async_copy(sum_ref, sum_hbm, sems.at[1]),
    ]
    for copy in copies:
        copy.start()
    for copy in copies:
        copy.wait()


def attend_to(
    steps, begun, ids_ref, q_ref, blocks, queries, held, top_ref, sum_ref, pair_ref, one_ref, full_ref, scores
):
    slot = lax.axis_index("group")
    hold(held, blocks)
    count = held.shape[2]
    for number, step in enumerate(steps):
        queries[number] = q_ref[place_across(slot, step)]

    if not begun:

        @pl.loop(0, len(steps))
        def _(number):
            sum_ref[number] = jnp.zeros_like(sum_ref[number])
            estimate(number, queries.at[number], blocks[0][0, pl.ds(0, HD), :], top_ref)

    sees = []
    full_length = jnp.int32(0)
    seen = []
    for number, step in enumerate(steps):
        rank = ids_ref[OWNERS[step](slot)]
        before = full_length
        row = []
        for block, group in enumerate(key_groups(slot)):
            see = (ids_ref[group] <= rank).astype(jnp.int32)
            full_ref[full_length] = 4 * number + block
            full_length = full_length + see
            if block > 1 or not begun:
                row.append((block, see))
        sees.append(row)
        seen.append(full_length > before)
    if begun:
        for copy in begun:
            copy.wait()
    add_seen(sees, held, queries, top_ref, sum_ref, pair_ref, one_ref, scores)

    inside = jnp.bool_(True)
    for number, some in enumerate(seen):
        totals = sum_ref[number, :, HD : HD + 1, :]
        good = (jnp.min(totals) > SMALL) & (jnp.max(totals) < LARGE)
        inside = inside & (good | jnp.logical_not(some))

    @pl.when(jnp.logical_not(inside))
    def _():
        top_ref[...] = jnp.full_like(top_ref, LOW)
        sum_ref[...] = jnp.zeros_like(sum_ref)
        halves = count // TILE

        @pl.loop(0, full_length * halves)
        def _(index):
            code = full_ref[index // halves]
            number, block = code // 4, code % 4
            half = index % halves
            k, v = keys_of([held.at[block]], count), values_of([held.at[block]], count)
            where = pl.ds(pl.multiple_of(half * TILE, TILE), TILE)
            s = scores_of(k, queries[number, where, :])
            old = top_ref[number, half]
            new = jnp.maximum(old, jnp.max(s, axis=0, keepdims=True))
            top_ref[number, half] = new
            sum_ref[number, half] = sum_ref[number, half] * jnp.exp2((old - new) * LOG2)
            mix(number, half, s, v, top_ref, sum_ref)


def attend_kernel(
    ids_ref, q_ref, b0, b1, b2, b3,
    out_ref, queries, held, top_ref, sum_ref, pair_ref, one_ref, full_ref, *scores,
):
    attend_to(
        (1, 2, 3), (), ids_ref, q_ref, (b0, b1, b2, b3),
        queries, held, top_ref, sum_ref, pair_ref, one_ref, full_ref, scores,
    )
    slot = lax.axis_index("group")
    count = held.shape[2]
    for number in range(3):
        place = place_across(slot, number + 1)

        @pl.loop(0, count // TILE)
        def _(half):
            def write(start, part):
                where = pl.ds(pl.multiple_of(half * TILE + start, HD), HD)
                out_ref[place, where, :] = part.astype(jnp.bfloat16)

            means(sum_ref[number, half], write)

        logs = log_sums(number, top_ref, sum_ref)
        high = logs.astype(jnp.bfloat16)
        rest = logs - high.astype(jnp.float32)
        mid = rest.astype(jnp.bfloat16)
        low = (rest - mid.astype(jnp.float32)).astype(jnp.bfloat16)
        tail = jnp.concatenate([high, mid, low, jnp.zeros_like(low)], axis=0)
        out_ref[place, pl.ds(count, 32), :] = tail


def own_kernel(
    ids_ref, q_ref, b0, b1, b2, b3, top_hbm, sum_hbm,
    out_ref, queries, held, top_ref, sum_ref, sems, pair_ref, one_ref, full_ref, *scores,
):
    copies = [
        pltpu.make_async_copy(top_hbm, top_ref, sems.at[0]),
        pltpu.make_async_copy(sum_hbm, sum_ref, sems.at[1]),
    ]
    for copy in copies:
        copy.start()
    attend_to(
        (0,), copies, ids_ref, q_ref, (b0, b1, b2, b3),
        queries, held, top_ref, sum_ref, pair_ref, one_ref, full_ref, scores,
    )
    count = held.shape[2]

    @pl.loop(0, count // TILE)
    def _(half):
        def write(start, part):
            out_ref[pl.ds(pl.multiple_of(half * TILE + start, HD), HD), :] = part

        means(sum_ref[0, half], write)

    out_ref[pl.ds(count, 8), :] = log_sums(0, top_ref, sum_ref)


def log_sums(place, top_ref, sum_ref):
    lines = []
    for half in range(top_ref.shape[1]):
        total = sum_ref[place, half, HD : HD + 1, :]
        logs = jnp.where(total > 0, jnp.log2(total) + top_ref[place, half] * LOG2, LOW)
        lines += [logs[:, start : start + HD] for start in range(0, TILE, HD)]
    lines.append(jnp.full((8 - len(lines), HD), LOW, jnp.float32))
    return jnp.concatenate(lines, axis=0)


def means(sums, write):
    for start in range(0, TILE, HD):
        total = sums[HD : HD + 1, start : start + HD]
        write(start, sums[:HD, start : start + HD] / jnp.where(total > 0, total, 1.0))


def cost(parts):
    return pl.CostEstimate(
        flops=parts * 4 * 768 * 768 * 128,
        bytes_accessed=parts * 2**19,
        transcendentals=parts * 768 * 768,
    )


def state(places, count):
    halves = count // TILE
    return [
        jax.ShapeDtypeStruct((places, halves, 1, TILE), jnp.float32),
        jax.ShapeDtypeStruct((places, halves, HD + 16, TILE), jnp.float32),
    ]


def scores_scratch(count):
    return [pltpu.VMEM((2 * count, TILE), jnp.float32)] * (count // TILE)


def first(group_ids, q, one, two):
    count = q.shape[1]
    return pl.pallas_call(
        first_kernel,
        in_specs=[SMEM] + [VMEM] * 3,
        out_specs=[HBM] * 2,
        out_shape=state(1, count),
        scratch_shapes=[
            pltpu.VMEM((2, 2, count, HD), jnp.bfloat16),
            *(pltpu.VMEM(one.shape, one.dtype) for one in state(1, count)),
            pltpu.SemaphoreType.DMA((2,)),
            pltpu.SMEM((4,), jnp.int32),
            pltpu.SMEM((4,), jnp.int32),
            *scores_scratch(count),
        ],
        compiler_params=PARAMS,
        cost_estimate=cost(2),
        name="first",
    )(group_ids, q, one, two)


def attend_scratch(places, count):
    return [
        pltpu.VMEM((places, count, HD), jnp.bfloat16),
        pltpu.VMEM((4, 2, count, HD), jnp.bfloat16),
        *(pltpu.VMEM(one.shape, one.dtype) for one in state(places, count)),
    ]


def lists(places):
    return [pltpu.SMEM((4 * places + 4,), jnp.int32)] * 3


def attend(group_ids, queries, blocks):
    count = queries.shape[1]
    return pl.pallas_call(
        attend_kernel,
        in_specs=[SMEM] + [VMEM] * 5,
        out_specs=VMEM,
        out_shape=jax.ShapeDtypeStruct((4, count + 32, HD), jnp.bfloat16),
        scratch_shapes=[*attend_scratch(3, count), *lists(3), *scores_scratch(count)],
        compiler_params=PARAMS,
        cost_estimate=cost(12),
        name="attend",
    )(group_ids, queries, *blocks)


def own(group_ids, queries, blocks, begun):
    count = queries.shape[1]
    return pl.pallas_call(
        own_kernel,
        in_specs=[SMEM] + [VMEM] * 5 + [HBM] * 2,
        out_specs=VMEM,
        out_shape=jax.ShapeDtypeStruct((count + 8, HD), jnp.float32),
        scratch_shapes=[
            *attend_scratch(1, count),
            pltpu.SemaphoreType.DMA((2,)),
            *lists(1),
            *scores_scratch(count),
        ],
        compiler_params=PARAMS,
        cost_estimate=cost(2),
        name="own",
    )(group_ids, queries, *blocks, *begun)


def cross_kernel(len_ref, in_ref, text_ref, out_hbm, c_ref, cross_ref, sem):
    def write_queries(where, piece):
        c_ref[where, :] = piece

    pairs_of(in_ref, 3, write_queries)
    pieces, _, texts, _ = text_ref.shape
    length = pieces * texts
    mask = lax.broadcasted_iota(jnp.int32, (length, 1), 0) < len_ref[0]
    k = text_ref[:, 0].reshape(length, HD)
    v = with_ones(text_ref[:, 1].reshape(length, HD).T)

    @pl.loop(0, c_ref.shape[0] // TILE)
    def _(half):
        queries = c_ref[pl.ds(pl.multiple_of(half * TILE, TILE), TILE), :]
        s = jnp.where(mask, scores_of(k, queries), LOW)
        top = jnp.max(s, axis=0, keepdims=True)
        p = jnp.exp2((s - top) * LOG2).astype(jnp.bfloat16)
        sums = jnp.dot(v, p, preferred_element_type=jnp.float32)

        def write(start, part):
            cross_ref[pl.ds(pl.multiple_of(half * TILE + start, HD), HD), :] = part

        means(sums, write)

    copy = pltpu.make_async_copy(cross_ref, out_hbm, sem)
    copy.start()
    copy.wait()


def cross_part(text_len, received, text):
    parts, _, rows, width = received.shape
    count = parts * rows
    return pl.pallas_call(
        cross_kernel,
        in_specs=[SMEM] + [VMEM] * 2,
        out_specs=HBM,
        out_shape=jax.ShapeDtypeStruct((count, width), jnp.float32),
        scratch_shapes=[
            pltpu.VMEM((count, width), jnp.bfloat16),
            pltpu.VMEM((count, width), jnp.float32),
            pltpu.SemaphoreType.DMA,
        ],
        compiler_params=PARAMS,
        cost_estimate=cost(2),
        name="cross",
    )(text_len, received, text)


def merge_kernel(
    own_hbm, cross_hbm, back_ref, gate_hbm, out_ref, own_ref, cross_ref, weight_ref, gate_ref, sems
):
    copies = [
        pltpu.make_async_copy(source, target, sems.at[number])
        for number, (source, target) in enumerate(
            ((own_hbm, own_ref), (cross_hbm, cross_ref), (gate_hbm, gate_ref))
        )
    ]
    for copy in copies:
        copy.start()
    slot = lax.axis_index("group")
    count = cross_ref.shape[0]
    received = [back_ref.at[place_across(slot, step)] for step in (1, 2, 3)]
    logs = []
    for ref in received:
        tail = ref[pl.ds(count, 32), :].astype(jnp.float32)
        logs.append(tail[0:8] + tail[8:16] + tail[16:24])
    for copy in copies:
        copy.wait()
    logs.append(own_ref[pl.ds(count, 8), :])
    best = functools.reduce(jnp.maximum, logs)
    weights = [jnp.exp2(line - best) for line in logs]
    total = functools.reduce(jnp.add, weights)
    for place, weight in enumerate(weights):
        weight_ref[place] = weight / total
    gate = jnp.broadcast_to(gate_ref[...], (HD, HD)).T

    @pl.loop(0, count // HD)
    def _(step):
        rows = pl.ds(pl.multiple_of(step * HD, HD), HD)
        mixed = weight_ref[3, pl.ds(step, 1), :] * own_ref[rows, :]
        for place, ref in enumerate(received):
            line = weight_ref[place, pl.ds(step, 1), :]
            mixed = mixed + line * ref[rows, :].astype(jnp.float32)
        out_ref[rows, :] = (gate * mixed + cross_ref[rows, :]).astype(jnp.bfloat16).T


def merge(mine, cross, back, gate):
    return pl.pallas_call(
        merge_kernel,
        in_specs=[HBM, HBM, VMEM, HBM],
        out_specs=VMEM,
        out_shape=jax.ShapeDtypeStruct(cross.shape, jnp.bfloat16),
        scratch_shapes=[
            pltpu.VMEM(mine.shape, jnp.float32),
            pltpu.VMEM(cross.shape, jnp.float32),
            pltpu.VMEM((4, 8, HD), jnp.float32),
            pltpu.VMEM(gate.shape, jnp.float32),
            pltpu.SemaphoreType.DMA((3,)),
        ],
        compiler_params=PARAMS,
        cost_estimate=cost(1),
        name="merge",
    )(mine, cross, back, gate)


def to_heads(array):
    return lax.all_to_all(array, "seq", split_axis=0, concat_axis=0, tiled=True)


def body(
    queries, keys, values, cross_queries, text_keys, text_values, group_gate, group_ids, text_len
):
    packed = pack(queries, keys, values, cross_queries)
    received = to_heads(packed)
    q, kv, text = unpack(received, text_keys, text_values)
    kv_core = swap(kv, core_of)
    kv_near = swap(kv, across_y1)
    begun = first(group_ids, q, kv, kv_core)
    q, kv_core = lax.optimization_barrier((q, kv_core))
    text, begun = lax.optimization_barrier((text, begun))
    text = lax.all_to_all(text, "group", split_axis=0, concat_axis=0, tiled=True)
    blocks = (kv, kv_core, kv_near, swap(kv_near, core_of))
    q = in_cluster(q)
    sent, q, text = lax.optimization_barrier((attend(group_ids, q, blocks), q, text))
    back = in_cluster(sent)
    mine = own(group_ids, q, blocks, begun)
    mixed = merge(mine, cross_part(text_len, received, text), back, group_gate)
    count = mixed.shape[0]
    heads = lax.axis_size("seq")
    mixed = to_heads(mixed.reshape(heads, count // heads, HD))
    return jnp.transpose(mixed, (1, 0, 2)).reshape(1, count // heads, heads * HD)


def solution(mesh):
    return jax.shard_map(
        body,
        mesh=mesh,
        in_specs=(
            P("group", "seq", None),
            P("group", "seq", None),
            P("group", "seq", None),
            P("group", "seq", None),
            P("group", "seq"),
            P("group", "seq"),
            P("group", "seq"),
            P(),
            P(),
        ),
        out_specs=P("group", "seq", None),
        check_vma=False,
    )
```

```python
import functools
import math

import jax
import jax.numpy as jnp
from jax import lax
from jax.experimental import pallas as pl
from jax.experimental.pallas import tpu as pltpu
from jax.sharding import PartitionSpec as P

HD = 128
LOG2 = math.log2(math.e) / math.sqrt(HD)
LOW = -1e30
VMEM = pl.BlockSpec(memory_space=pltpu.VMEM)
SMEM = pl.BlockSpec(memory_space=pltpu.SMEM)
HBM = pl.BlockSpec(memory_space=pltpu.HBM)
PARAMS = pltpu.CompilerParams(vmem_limit_bytes=14 * 2**20)


SMALL, LARGE = 2.0**-60, 2.0**90
TILE = 384


def core_of(i):
    return i + 1 - 2 * (i % 2)


def across_x(i):
    return (i + 8) % 16


def across_y1(i):
    y = (i // 2) % 4
    return i + 2 * (1 - 2 * (y % 2))


def across_y2(i):
    y = (i // 2) % 4
    return (i // 8) * 8 + ((y + 2 * (y % 2) + 3) % 4) * 2 + i % 2


def across_xy2(i):
    return across_x(across_y2(i))


CLUSTERS = [
    [i, across_x(i), across_y2(i), across_xy2(i)] for i in (2, 3, 6, 7)
]
OWNERS = (lambda i: i, across_x, across_y2, across_xy2)


def place_of(i):
    y = (i // 2) % 4
    return i // 8 + 2 * ((y + 1) % 2)


def place_across(i, step):
    place = place_of(i)
    x, y = place % 2, place // 2
    if step % 2:
        x = 1 - x
    if step // 2:
        y = 1 - y
    return x + 2 * y


def in_cluster(array):
    return lax.all_to_all(
        array, "group", split_axis=0, concat_axis=0, axis_index_groups=CLUSTERS, tiled=True
    )


def swap(array, partner):
    return lax.ppermute(array, "group", [(i, partner(i)) for i in range(16)])


CHUNKS = 4


def pack_kernel(q_hbm, k_hbm, v_hbm, c_hbm, out_ref, held, sems):
    sources = (q_hbm, k_hbm, v_hbm, c_hbm)
    heads = out_ref.shape[0]
    chunk = heads // CHUNKS * HD
    copies = []
    for slot, ref in enumerate(sources):
        for part in range(CHUNKS):
            where = pl.ds(part * chunk, chunk)
            copy = pltpu.make_async_copy(
                ref.at[0, :, where], held.at[slot, :, where], sems.at[slot, part]
            )
            copy.start()
            copies.append(copy)
    for slot in range(len(sources)):
        for part in range(CHUNKS):
            copies[slot * CHUNKS + part].wait()
            for head in range(part * heads // CHUNKS, (part + 1) * heads // CHUNKS):
                out_ref[head, slot] = held[slot, :, head * HD : (head + 1) * HD]


def pack(queries, keys, values, cross_queries):
    rows, width = queries.shape[1:]
    heads = width // HD
    return pl.pallas_call(
        pack_kernel,
        in_specs=[pl.BlockSpec(memory_space=pl.ANY)] * 4,
        out_specs=VMEM,
        out_shape=jax.ShapeDtypeStruct((heads, 4, rows, HD), jnp.bfloat16),
        scratch_shapes=[
            pltpu.VMEM((4, rows, width), jnp.bfloat16),
            pltpu.SemaphoreType.DMA((4, CHUNKS)),
        ],
        compiler_params=pltpu.CompilerParams(vmem_limit_bytes=56 * 2**20),
        name="pack",
    )(queries, keys, values, cross_queries)


def pairs_of(in_ref, slot, write):
    parts, _, rows, _ = in_ref.shape

    @pl.loop(0, parts // 2)
    def _(part):
        where = pl.ds(pl.multiple_of(part * 2 * rows, 16), 2 * rows)
        pieces = [in_ref[2 * part, slot], in_ref[2 * part + 1, slot]]
        write(where, jnp.concatenate(pieces, axis=0))


def unpack_kernel(in_ref, tk_hbm, tv_hbm, q_ref, kv_ref, all_ref, v_ref, text_ref, sems):
    copies = [
        pltpu.make_async_copy(ref, text_ref.at[side], sems.at[side])
        for side, ref in enumerate((tk_hbm, tv_hbm))
    ]
    for copy in copies:
        copy.start()

    def into(ref):
        def write(where, piece):
            ref[where, :] = piece

        return write

    count = v_ref.shape[0]

    def write_queries(where, piece):
        for place in range(q_ref.shape[0]):
            q_ref[place, where, :] = piece

    pairs_of(in_ref, 0, write_queries)
    pairs_of(in_ref, 1, into(kv_ref.at[0]))
    pairs_of(in_ref, 2, into(v_ref))

    @pl.loop(0, count // HD)
    def _(block):
        where = pl.ds(pl.multiple_of(block * HD, HD), HD)
        kv_ref[1, where, :] = v_ref[where, :].T

    for copy in copies:
        copy.wait()
    for place in range(all_ref.shape[0]):
        all_ref[place] = text_ref[...]


def unpack(received, text_keys, text_values):
    parts, _, rows, width = received.shape
    count = parts * rows
    return pl.pallas_call(
        unpack_kernel,
        in_specs=[VMEM] + [HBM] * 2,
        out_specs=[VMEM] * 3,
        out_shape=[
            jax.ShapeDtypeStruct((4, count, width), jnp.bfloat16),
            jax.ShapeDtypeStruct((2, count, width), jnp.bfloat16),
            jax.ShapeDtypeStruct((16, 2) + text_keys.shape, jnp.bfloat16),
        ],
        scratch_shapes=[
            pltpu.VMEM((count, width), jnp.bfloat16),
            pltpu.VMEM((2,) + text_keys.shape, jnp.bfloat16),
            pltpu.SemaphoreType.DMA((2,)),
        ],
        compiler_params=PARAMS,
        name="unpack",
    )(received, text_keys, text_values)


def scores_of(k, q):
    return lax.dot_general(
        k, q, (((1,), (1,)), ((), ())), preferred_element_type=jnp.float32
    )


def with_ones(v):
    return jnp.concatenate([v, jnp.ones((16, v.shape[1]), v.dtype)], axis=0)


def features_first(v_blocks):
    count = v_blocks.shape[0] // HD
    return jnp.concatenate([v_blocks[i * HD : (i + 1) * HD] for i in range(count)], axis=1)


def key_groups(slot):
    near = across_y1(slot)
    return slot, core_of(slot), near, core_of(near)


def keys_of(blocks, count):
    return jnp.concatenate([block[0, pl.ds(0, count), :] for block in blocks], axis=0)


def values_of(blocks, count):
    parts = [features_first(block[1, pl.ds(0, count), :]) for block in blocks]
    return with_ones(jnp.concatenate(parts, axis=1))


def half_of(q_ref, half):
    return q_ref[pl.ds(half * TILE, TILE), :]


def hold(held, blocks):
    @pl.loop(0, held.shape[2] // 32)
    def _(step):
        rows = pl.ds(pl.multiple_of(step * 32, 32), 32)
        for number, block in enumerate(blocks):
            for side in range(2):
                held[number, side, rows, :] = block[side, rows, :]


def mix(place, half, s, v, top_ref, sum_ref):
    p = jnp.exp2((s - top_ref[place, half]) * LOG2).astype(jnp.bfloat16)
    sum_ref[place, half] += jnp.dot(v, p, preferred_element_type=jnp.float32)


def estimate(place, q_ref, keys, top_ref):
    for half in range(q_ref.shape[0] // TILE):
        s = scores_of(keys, half_of(q_ref, half))
        top_ref[place, half] = jnp.max(s, axis=0, keepdims=True)


def add_listed(length, list_ref, width, held, queries, top_ref, sum_ref, scores):
    count = held.shape[2]
    last = len(scores) - 1
    scores = [ref.at[pl.ds(0, width * count), :] for ref in scores]

    def item(index):
        code = list_ref[index]
        blocks = [held.at[code // 4**digit % 4] for digit in range(width)]
        return code // 4**width, blocks

    @pl.when(length > 0)
    def _():
        place, blocks = item(0)
        scores[0][...] = scores_of(keys_of(blocks, count), half_of(queries.at[place], 0))

        @pl.loop(0, length)
        def _(index):
            place, blocks = item(index)
            k, v = keys_of(blocks, count), values_of(blocks, count)
            after, blocks = item(jnp.minimum(index + 1, length - 1))
            for tile in range(last):
                scores[tile + 1][...] = scores_of(k, half_of(queries.at[place], tile + 1))
                mix(place, tile, scores[tile][...], v, top_ref, sum_ref)
            final = scores[last][...]
            scores[0][...] = scores_of(keys_of(blocks, count), half_of(queries.at[after], 0))
            mix(place, last, final, v, top_ref, sum_ref)


def add_seen(sees, held, queries, top_ref, sum_ref, pair_ref, one_ref, scores):
    pairs, ones = jnp.int32(0), jnp.int32(0)
    for place, row in enumerate(sees):
        waiting, waits = jnp.int32(0), jnp.int32(0)
        for block, see in row:
            pair_ref[pairs] = 16 * place + 4 * waiting + block
            pairs = pairs + see * waits
            waiting = jnp.where(waits > 0, waiting, block)
            waits = (waits + see) % 2
            waiting = jnp.where(waits > 0, waiting, 0)
        one_ref[ones] = 4 * place + waiting
        ones = ones + waits
    add_listed(pairs, pair_ref, 2, held, queries, top_ref, sum_ref, scores)
    add_listed(ones, one_ref, 1, held, queries, top_ref, sum_ref, scores)


def first_kernel(
    ids_ref, q4_ref, one, two, top_hbm, sum_hbm, held, top_ref, sum_ref, sems, pair_ref, one_ref, *scores
):
    slot = lax.axis_index("group")
    q_ref = q4_ref.at[0]
    hold(held, (one, two))
    sum_ref[...] = jnp.zeros_like(sum_ref)
    estimate(0, q_ref, one[0, pl.ds(0, HD), :], top_ref)
    see = (ids_ref[core_of(slot)] <= ids_ref[slot]).astype(jnp.int32)
    sees = [[(0, jnp.int32(1)), (1, see)]]
    add_seen(sees, held, q4_ref, top_ref, sum_ref, pair_ref, one_ref, scores)
    copies = [
        pltpu.make_async_copy(top_ref, top_hbm, sems.at[0]),
        pltpu.make_async_copy(sum_ref, sum_hbm, sems.at[1]),
    ]
    for copy in copies:
        copy.start()
    for copy in copies:
        copy.wait()


def attend_to(
    steps, begun, ids_ref, q_ref, blocks, queries, held, top_ref, sum_ref, pair_ref, one_ref, full_ref, scores
):
    slot = lax.axis_index("group")
    hold(held, blocks)
    count = held.shape[2]
    for number, step in enumerate(steps):
        queries[number] = q_ref[place_across(slot, step)]

    if not begun:

        @pl.loop(0, len(steps))
        def _(number):
            sum_ref[number] = jnp.zeros_like(sum_ref[number])
            estimate(number, queries.at[number], blocks[0][0, pl.ds(0, HD), :], top_ref)

    sees = []
    full_length = jnp.int32(0)
    seen = []
    for number, step in enumerate(steps):
        rank = ids_ref[OWNERS[step](slot)]
        before = full_length
        row = []
        for block, group in enumerate(key_groups(slot)):
            see = (ids_ref[group] <= rank).astype(jnp.int32)
            full_ref[full_length] = 4 * number + block
            full_length = full_length + see
            if block > 1 or not begun:
                row.append((block, see))
        sees.append(row)
        seen.append(full_length > before)
    if begun:
        for copy in begun:
            copy.wait()
    add_seen(sees, held, queries, top_ref, sum_ref, pair_ref, one_ref, scores)

    inside = jnp.bool_(True)
    for number, some in enumerate(seen):
        totals = sum_ref[number, :, HD : HD + 1, :]
        good = (jnp.min(totals) > SMALL) & (jnp.max(totals) < LARGE)
        inside = inside & (good | jnp.logical_not(some))

    @pl.when(jnp.logical_not(inside))
    def _():
        top_ref[...] = jnp.full_like(top_ref, LOW)
        sum_ref[...] = jnp.zeros_like(sum_ref)
        halves = count // TILE

        @pl.loop(0, full_length * halves)
        def _(index):
            code = full_ref[index // halves]
            number, block = code // 4, code % 4
            half = index % halves
            k, v = keys_of([held.at[block]], count), values_of([held.at[block]], count)
            where = pl.ds(pl.multiple_of(half * TILE, TILE), TILE)
            s = scores_of(k, queries[number, where, :])
            old = top_ref[number, half]
            new = jnp.maximum(old, jnp.max(s, axis=0, keepdims=True))
            top_ref[number, half] = new
            sum_ref[number, half] = sum_ref[number, half] * jnp.exp2((old - new) * LOG2)
            mix(number, half, s, v, top_ref, sum_ref)


def attend_kernel(
    ids_ref, q_ref, b0, b1, b2, b3,
    out_ref, queries, held, top_ref, sum_ref, pair_ref, one_ref, full_ref, *scores,
):
    attend_to(
        (1, 2, 3), (), ids_ref, q_ref, (b0, b1, b2, b3),
        queries, held, top_ref, sum_ref, pair_ref, one_ref, full_ref, scores,
    )
    slot = lax.axis_index("group")
    count = held.shape[2]
    for number in range(3):
        place = place_across(slot, number + 1)

        @pl.loop(0, count // TILE)
        def _(half):
            def write(start, part):
                where = pl.ds(pl.multiple_of(half * TILE + start, HD), HD)
                out_ref[place, where, :] = part.astype(jnp.bfloat16)

            means(sum_ref[number, half], write)

        logs = log_sums(number, top_ref, sum_ref)
        high = logs.astype(jnp.bfloat16)
        rest = logs - high.astype(jnp.float32)
        mid = rest.astype(jnp.bfloat16)
        low = (rest - mid.astype(jnp.float32)).astype(jnp.bfloat16)
        tail = jnp.concatenate([high, mid, low, jnp.zeros_like(low)], axis=0)
        out_ref[place, pl.ds(count, 32), :] = tail


def own_kernel(
    ids_ref, q_ref, b0, b1, b2, b3, cross_ref, top_hbm, sum_hbm,
    out_ref, queries, held, top_ref, sum_ref, sems, pair_ref, one_ref, full_ref, *scores,
):
    copies = [
        pltpu.make_async_copy(top_hbm, top_ref, sems.at[0]),
        pltpu.make_async_copy(sum_hbm, sum_ref, sems.at[1]),
    ]
    for copy in copies:
        copy.start()
    attend_to(
        (0,), copies, ids_ref, q_ref, (b0, b1, b2, b3),
        queries, held, top_ref, sum_ref, pair_ref, one_ref, full_ref, scores,
    )
    count = held.shape[2]

    @pl.loop(0, count // TILE)
    def _(half):
        def write(start, part):
            where = pl.ds(pl.multiple_of(half * TILE + start, HD), HD)
            out_ref[0, where, :] = cross_ref[where, :]
            out_ref[1, where, :] = part

        means(sum_ref[0, half], write)

    out_ref[1, pl.ds(count, 8), :] = log_sums(0, top_ref, sum_ref)


def log_sums(place, top_ref, sum_ref):
    lines = []
    for half in range(top_ref.shape[1]):
        total = sum_ref[place, half, HD : HD + 1, :]
        logs = jnp.where(total > 0, jnp.log2(total) + top_ref[place, half] * LOG2, LOW)
        lines += [logs[:, start : start + HD] for start in range(0, TILE, HD)]
    lines.append(jnp.full((8 - len(lines), HD), LOW, jnp.float32))
    return jnp.concatenate(lines, axis=0)


def means(sums, write):
    for start in range(0, TILE, HD):
        total = sums[HD : HD + 1, start : start + HD]
        write(start, sums[:HD, start : start + HD] / jnp.where(total > 0, total, 1.0))


def cost(parts):
    return pl.CostEstimate(
        flops=parts * 4 * 768 * 768 * 128,
        bytes_accessed=parts * 2**19,
        transcendentals=parts * 768 * 768,
    )


def state(places, count):
    halves = count // TILE
    return [
        jax.ShapeDtypeStruct((places, halves, 1, TILE), jnp.float32),
        jax.ShapeDtypeStruct((places, halves, HD + 16, TILE), jnp.float32),
    ]


def scores_scratch(count):
    return [pltpu.VMEM((2 * count, TILE), jnp.float32)] * (count // TILE)


def first(group_ids, q, one, two):
    count = q.shape[1]
    return pl.pallas_call(
        first_kernel,
        in_specs=[SMEM] + [VMEM] * 3,
        out_specs=[HBM] * 2,
        out_shape=state(1, count),
        scratch_shapes=[
            pltpu.VMEM((2, 2, count, HD), jnp.bfloat16),
            *(pltpu.VMEM(one.shape, one.dtype) for one in state(1, count)),
            pltpu.SemaphoreType.DMA((2,)),
            pltpu.SMEM((4,), jnp.int32),
            pltpu.SMEM((4,), jnp.int32),
            *scores_scratch(count),
        ],
        compiler_params=PARAMS,
        cost_estimate=cost(2),
        name="first",
    )(group_ids, q, one, two)


def attend_scratch(places, count):
    return [
        pltpu.VMEM((places, count, HD), jnp.bfloat16),
        pltpu.VMEM((4, 2, count, HD), jnp.bfloat16),
        *(pltpu.VMEM(one.shape, one.dtype) for one in state(places, count)),
    ]


def lists(places):
    return [pltpu.SMEM((4 * places + 4,), jnp.int32)] * 3


def attend(group_ids, queries, blocks):
    count = queries.shape[1]
    return pl.pallas_call(
        attend_kernel,
        in_specs=[SMEM] + [VMEM] * 5,
        out_specs=VMEM,
        out_shape=jax.ShapeDtypeStruct((4, count + 32, HD), jnp.bfloat16),
        scratch_shapes=[*attend_scratch(3, count), *lists(3), *scores_scratch(count)],
        compiler_params=PARAMS,
        cost_estimate=cost(12),
        name="attend",
    )(group_ids, queries, *blocks)


def own(group_ids, queries, blocks, cross, begun):
    count = queries.shape[1]
    return pl.pallas_call(
        own_kernel,
        in_specs=[SMEM] + [VMEM] * 6 + [HBM] * 2,
        out_specs=VMEM,
        out_shape=jax.ShapeDtypeStruct((2, count + 8, HD), jnp.float32),
        scratch_shapes=[
            *attend_scratch(1, count),
            pltpu.SemaphoreType.DMA((2,)),
            *lists(1),
            *scores_scratch(count),
        ],
        compiler_params=PARAMS,
        cost_estimate=cost(2),
        name="own",
    )(group_ids, queries, *blocks, cross, *begun)


def cross_kernel(len_ref, in_ref, text_ref, out_hbm, c_ref, cross_ref, sem):
    def write_queries(where, piece):
        c_ref[where, :] = piece

    pairs_of(in_ref, 3, write_queries)
    pieces, _, texts, _ = text_ref.shape
    length = pieces * texts
    mask = lax.broadcasted_iota(jnp.int32, (length, 1), 0) < len_ref[0]
    k = text_ref[:, 0].reshape(length, HD)
    v = with_ones(text_ref[:, 1].reshape(length, HD).T)

    @pl.loop(0, c_ref.shape[0] // TILE)
    def _(half):
        queries = c_ref[pl.ds(pl.multiple_of(half * TILE, TILE), TILE), :]
        s = jnp.where(mask, scores_of(k, queries), LOW)
        top = jnp.max(s, axis=0, keepdims=True)
        p = jnp.exp2((s - top) * LOG2).astype(jnp.bfloat16)
        sums = jnp.dot(v, p, preferred_element_type=jnp.float32)

        def write(start, part):
            cross_ref[pl.ds(pl.multiple_of(half * TILE + start, HD), HD), :] = part

        means(sums, write)

    copy = pltpu.make_async_copy(cross_ref, out_hbm, sem)
    copy.start()
    copy.wait()


def cross_part(text_len, received, text):
    parts, _, rows, width = received.shape
    count = parts * rows
    return pl.pallas_call(
        cross_kernel,
        in_specs=[SMEM] + [VMEM] * 2,
        out_specs=HBM,
        out_shape=jax.ShapeDtypeStruct((count, width), jnp.float32),
        scratch_shapes=[
            pltpu.VMEM((count, width), jnp.bfloat16),
            pltpu.VMEM((count, width), jnp.float32),
            pltpu.SemaphoreType.DMA,
        ],
        compiler_params=PARAMS,
        cost_estimate=cost(2),
        name="cross",
    )(text_len, received, text)


def merge_kernel(mine_hbm, back_ref, gate_hbm, out_ref, mine_ref, weight_ref, gate_ref, sems):
    copies = [
        pltpu.make_async_copy(mine_hbm, mine_ref, sems.at[0]),
        pltpu.make_async_copy(gate_hbm, gate_ref, sems.at[1]),
    ]
    for copy in copies:
        copy.start()
    slot = lax.axis_index("group")
    count = out_ref.shape[0]
    received = [back_ref.at[place_across(slot, step)] for step in (1, 2, 3)]
    logs = []
    for ref in received:
        tail = ref[pl.ds(count, 32), :].astype(jnp.float32)
        logs.append(tail[0:8] + tail[8:16] + tail[16:24])
    for copy in copies:
        copy.wait()
    logs.append(mine_ref[1, pl.ds(count, 8), :])
    best = functools.reduce(jnp.maximum, logs)
    weights = [jnp.exp2(line - best) for line in logs]
    total = functools.reduce(jnp.add, weights)
    for place, weight in enumerate(weights):
        weight_ref[place] = weight / total
    gate = jnp.broadcast_to(gate_ref[...], (HD, HD)).T

    @pl.loop(0, count // HD)
    def _(step):
        rows = pl.ds(pl.multiple_of(step * HD, HD), HD)
        mixed = weight_ref[3, pl.ds(step, 1), :] * mine_ref[1, rows, :]
        for place, ref in enumerate(received):
            line = weight_ref[place, pl.ds(step, 1), :]
            mixed = mixed + line * ref[rows, :].astype(jnp.float32)
        out_ref[rows, :] = (gate * mixed + mine_ref[0, rows, :]).astype(jnp.bfloat16).T


def merge(mine, back, gate):
    return pl.pallas_call(
        merge_kernel,
        in_specs=[HBM, VMEM, HBM],
        out_specs=VMEM,
        out_shape=jax.ShapeDtypeStruct((mine.shape[1] - 8, HD), jnp.bfloat16),
        scratch_shapes=[
            pltpu.VMEM(mine.shape, jnp.float32),
            pltpu.VMEM((4, 8, HD), jnp.float32),
            pltpu.VMEM(gate.shape, jnp.float32),
            pltpu.SemaphoreType.DMA((2,)),
        ],
        compiler_params=PARAMS,
        cost_estimate=cost(1),
        name="merge",
    )(mine, back, gate)


def to_heads(array):
    return lax.all_to_all(array, "seq", split_axis=0, concat_axis=0, tiled=True)


def body(
    queries, keys, values, cross_queries, text_keys, text_values, group_gate, group_ids, text_len
):
    packed = pack(queries, keys, values, cross_queries)
    received = to_heads(packed)
    q, kv, text = unpack(received, text_keys, text_values)
    kv_core = swap(kv, core_of)
    kv_near = swap(kv, across_y1)
    begun = first(group_ids, q, kv, kv_core)
    q, kv_core = lax.optimization_barrier((q, kv_core))
    text, begun = lax.optimization_barrier((text, begun))
    text = lax.all_to_all(text, "group", split_axis=0, concat_axis=0, tiled=True)
    blocks = (kv, kv_core, kv_near, swap(kv_near, core_of))
    q = in_cluster(q)
    sent, q, text = lax.optimization_barrier((attend(group_ids, q, blocks), q, text))
    back = in_cluster(sent)
    mine = own(group_ids, q, blocks, cross_part(text_len, received, text), begun)
    mixed = merge(mine, back, group_gate)
    count = mixed.shape[0]
    heads = lax.axis_size("seq")
    mixed = to_heads(mixed.reshape(heads, count // heads, HD))
    return jnp.transpose(mixed, (1, 0, 2)).reshape(1, count // heads, heads * HD)


def solution(mesh):
    return jax.shard_map(
        body,
        mesh=mesh,
        in_specs=(
            P("group", "seq", None),
            P("group", "seq", None),
            P("group", "seq", None),
            P("group", "seq", None),
            P("group", "seq"),
            P("group", "seq"),
            P("group", "seq"),
            P(),
            P(),
        ),
        out_specs=P("group", "seq", None),
        check_vma=False,
    )
```
